256 devices in a mesh: dp: 32 (over z, y), tensor: 8 (over x, core).
Axes of the slice: x: 4, y: 4, z: 8, core: 2. Of those that a mesh axis runs over, the one named last changes fastest.
Arguments:
- cont_q: bfloat16 [640, 64, 8192], P('dp', None, 'tensor'), may hold values from -6 to 6
- cont_k: bfloat16 [640, 64, 1024], P('dp', None, 'tensor'), may hold values from -6 to 6
- cont_v: bfloat16 [640, 64, 1024], P('dp', None, 'tensor'), may hold values from -6 to 6
- out_grad: bfloat16 [640, 64, 8192], P('dp', None, 'tensor'), may hold values from -6 to 6
- prompt_k: bfloat16 [160, 128, 1024], P('dp', 'tensor'), may hold values from -6 to 6
- prompt_v: bfloat16 [160, 128, 1024], P('dp', 'tensor'), may hold values from -6 to 6
- cont_len: int32 [640], P('dp'), may hold values from 16 to 64, as said below
- cont_prompt: int32 [640], replicated, may hold values from 0 to 159, as said below
Outputs:
- attn_out: bfloat16 [640, 64, 8192], P('dp', None, 'tensor')
- grad_q: bfloat16 [640, 64, 8192], P('dp', None, 'tensor')
- grad_k: bfloat16 [640, 64, 1024], P('dp', None, 'tensor')
- grad_v: bfloat16 [640, 64, 1024], P('dp', None, 'tensor')
- grad_prompt_k: float32 [160, 128, 1024], P('dp', 'tensor')
- grad_prompt_v: float32 [160, 128, 1024], P('dp', 'tensor')
The draws below stay inside these ranges and needn't reach their ends.
Inputs may be any that keep to these rules, and one draw needn't show every extreme that they name: `cont_len`: each index of dp holds some slot of length 64. `cont_prompt`: prompt p is owned by index p // 5 of dp. Each prompt is continued by exactly 4 slots, on 4 different indices of dp. The slots of one index of dp name at most 1 different prompts of any one owner, and some index reaches 1.
All inputs are finite; a program needn't handle non-finite values.
Results may differ from the reference program's by a relative error of at most 0.012.
Values may be sent and summed in bfloat16 or wider, within the bound.
A program may use at most 128 MiB of HBM per device.

```python
import jax
import jax.numpy as jnp
from jax import lax

QH = 64
KVH = 8
HD = 128
PLEN = 128
MAXLEN = 64
GROUP = 4
P_DEV = 5
PROMPTS = 160
CONT_DEV = 20
CONTS = 640
N_DP = 32


def draw_cont_q(key, part):
    key = jax.random.fold_in(key, 21)
    array_shape = (CONTS, MAXLEN, QH * HD)
    values = jnp.clip(jax.random.normal(key, array_shape, jnp.float32), -6.0, 6.0)
    return values.astype(jnp.bfloat16)


def draw_cont_k(key, part):
    key = jax.random.fold_in(key, 22)
    array_shape = (CONTS, MAXLEN, KVH * HD)
    values = jnp.clip(jax.random.normal(key, array_shape, jnp.float32), -6.0, 6.0)
    return values.astype(jnp.bfloat16)


def draw_cont_len(key, part):
    key = jax.random.fold_in(key, 31)
    lengths = jax.random.randint(jax.random.fold_in(key, 1), (CONTS,), MAXLEN // 4, MAXLEN + 1)
    dev_count = CONTS // CONT_DEV
    longest = jax.random.randint(jax.random.fold_in(key, 2), (dev_count,), 0, CONT_DEV)
    targets = jnp.arange(dev_count) * CONT_DEV + longest
    filled = jnp.any(jnp.arange(CONTS)[:, None] == targets[None, :], axis=1)
    return jnp.where(filled, MAXLEN, lengths).astype(jnp.int32)


def place_front(values, wanted, position):
    where_now = jnp.argmax((values == wanted).astype(jnp.int32))
    held = values[position]
    values = values.at[where_now].set(held)
    return values.at[position].set(wanted)


def draw_cont_prompt(key, part):
    key = jax.random.fold_in(key, 41)
    dev_count = CONTS // CONT_DEV
    offsets = jax.random.permutation(jax.random.fold_in(key, 1), dev_count)
    offsets = place_front(offsets, 1, 0)
    offsets = place_front(offsets, dev_count // 2, 1)
    slot_types = jnp.arange(CONT_DEV)
    shifts = offsets[slot_types % dev_count]
    receivers = jnp.arange(dev_count)[:, None]
    by_type = (receivers - shifts[None, :]) % dev_count * P_DEV + slot_types[None, :] // GROUP
    order_keys = jax.random.split(jax.random.fold_in(key, 2), dev_count)
    orders = jax.vmap(lambda order_key: jax.random.permutation(order_key, CONT_DEV))(order_keys)
    inverse = jnp.argsort(orders, axis=1)
    placed = jnp.take_along_axis(by_type, inverse, axis=1)
    return placed.reshape(-1).astype(jnp.int32)


def steps_of(own_key, extent, shards, low, largest):
    factor_of = 1.0
    for dim, parts in shards:
        draws = jax.random.uniform(jax.random.fold_in(jax.random.fold_in(own_key, 6), dim), (parts,), jnp.float32, low / len(shards), largest / len(shards))
        factor_of = factor_of * jnp.repeat(jnp.exp(draws), extent[dim] // parts).reshape((-1,) + (1,) * (len(extent) - 1 - dim))
    return factor_of


def normal_values(key, dims, spread, limit, cuts=(), dtype=jnp.bfloat16):
    result = spread * jax.random.normal(key, dims, jnp.float32)
    if cuts:
        result = result * steps_of(key, dims, cuts, -0.22, 0.18)
    return jnp.clip(result, -limit, limit).astype(dtype)


def setup_inputs(seed: int = 0) -> dict:
    seeds = jax.random.split(jax.random.key(seed), 9)
    cont_q = draw_cont_q(jax.random.fold_in(seeds[8], 71), 0)
    cont_k = draw_cont_k(jax.random.fold_in(seeds[8], 71), 0)
    cont_v = normal_values(seeds[2], (CONTS, MAXLEN, KVH * HD), 1.0, 6.0, ((0, 32), (2, 8)))
    out_grad = normal_values(seeds[3], (CONTS, MAXLEN, QH * HD), 1.0, 6.0, ((0, 32), (2, 8)))
    prompt_k = normal_values(seeds[4], (PROMPTS, PLEN, KVH * HD), 1.0, 6.0, ((0, 32), (1, 8)))
    prompt_v = normal_values(seeds[5], (PROMPTS, PLEN, KVH * HD), 1.0, 6.0, ((0, 32), (1, 8)))
    cont_len = draw_cont_len(jax.random.fold_in(seeds[8], 71), 0)
    cont_prompt = draw_cont_prompt(jax.random.fold_in(seeds[8], 71), 0)
    return dict(cont_q=cont_q, cont_k=cont_k, cont_v=cont_v, out_grad=out_grad, prompt_k=prompt_k, prompt_v=prompt_v, cont_len=cont_len, cont_prompt=cont_prompt)


def attend_slot(inputs):
    query, own_k, own_v, pre_k, pre_v, grad_out, length = inputs
    seq_len = query.shape[0]
    prefix_len = pre_k.shape[0]
    key_count = prefix_len + seq_len
    group_size = QH // KVH
    score_scale = 1.0 / jnp.sqrt(jnp.float32(HD))
    queries = query.astype(jnp.float32).reshape(seq_len, KVH, group_size, HD)
    all_keys = jnp.concatenate((pre_k, own_k), axis=0).astype(jnp.float32).reshape(key_count, KVH, HD)
    all_values = jnp.concatenate((pre_v, own_v), axis=0).astype(jnp.float32).reshape(key_count, KVH, HD)
    scores = jnp.einsum('lhgd,khd->hglk', queries, all_keys) * score_scale
    row_index = lax.broadcasted_iota(jnp.int32, (seq_len, key_count), 0)
    col_index = lax.broadcasted_iota(jnp.int32, (seq_len, key_count), 1)
    scores = jnp.where(col_index <= row_index + prefix_len, scores, -jnp.inf)
    row_max = lax.optimization_barrier(jnp.max(scores, axis=-1, keepdims=True))
    exponent = jnp.exp(scores - row_max)
    probability = exponent / lax.optimization_barrier(jnp.sum(exponent, axis=-1, keepdims=True))
    weights = probability.astype(jnp.bfloat16).astype(jnp.float32)
    valid_rows = (jnp.arange(seq_len) < length).astype(jnp.float32)[:, None, None, None]
    attended = jnp.einsum('hglk,khd->lhgd', weights, all_values) * valid_rows
    masked = grad_out.reshape(seq_len, KVH, group_size, HD) * valid_rows.astype(jnp.bfloat16)
    masked = masked.astype(jnp.float32)
    dweights = jnp.einsum('lhgd,khd->hglk', masked, all_values)
    row_delta = lax.optimization_barrier(jnp.sum(probability * dweights, axis=-1, keepdims=True))
    dscores = (probability * (dweights - row_delta) * score_scale).astype(jnp.bfloat16).astype(jnp.float32)
    dquery = jnp.einsum('hglk,khd->lhgd', dscores, all_keys)
    dkey = jnp.einsum('hglk,lhgd->khd', dscores, queries).reshape(key_count, KVH * HD)
    dvalue = jnp.einsum('hglk,lhgd->khd', weights, masked).reshape(key_count, KVH * HD)
    return (attended.reshape(seq_len, QH * HD).astype(jnp.bfloat16), dquery.reshape(seq_len, QH * HD).astype(jnp.bfloat16), dkey[prefix_len:].astype(jnp.bfloat16), dvalue[prefix_len:].astype(jnp.bfloat16), dkey[:prefix_len], dvalue[:prefix_len])

def reference(cont_q, cont_k, cont_v, out_grad, prompt_k, prompt_v, cont_len, cont_prompt):
    pre_k = jnp.take(prompt_k, cont_prompt, axis=0)
    pre_v = jnp.take(prompt_v, cont_prompt, axis=0)
    attn_out, grad_q, grad_k, grad_v, pre_dk, pre_dv = lax.map(attend_slot, (cont_q, cont_k, cont_v, pre_k, pre_v, out_grad, cont_len))
    hosted = cont_prompt.reshape(N_DP, CONT_DEV)
    part_k = pre_dk.reshape(N_DP, CONT_DEV, PLEN, KVH * HD)
    part_v = pre_dv.reshape(N_DP, CONT_DEV, PLEN, KVH * HD)

    def add_device(carry, item):
        prompt_ids, slot_k, slot_v = item
        sum_k = jax.ops.segment_sum(slot_k, prompt_ids, num_segments=PROMPTS)
        sum_v = jax.ops.segment_sum(slot_v, prompt_ids, num_segments=PROMPTS)
        round_k, round_v = lax.optimization_barrier((sum_k.astype(jnp.bfloat16), sum_v.astype(jnp.bfloat16)))
        return ((carry[0] + round_k.astype(jnp.float32), carry[1] + round_v.astype(jnp.float32)), None)
    zeros = jnp.zeros((PROMPTS, PLEN, KVH * HD), jnp.float32)
    totals, unused = lax.scan(add_device, (zeros, zeros), (hosted, part_k, part_v))
    return (attn_out, grad_q, grad_k, grad_v, totals[0], totals[1])
```

```python
import functools
import math

import jax
import jax.numpy as jnp
from jax import lax
from jax.experimental import pallas as pl
from jax.experimental.pallas import tpu as pltpu
from jax.sharding import PartitionSpec as P

HD = 128
NY = 4
NEG = -1e30
MESH = pl.DeviceIdType.MESH
BF16 = jnp.bfloat16
F32 = jnp.float32


def coordinates(n_dp, n_t):
    dp = lax.axis_index("dp")
    t = lax.axis_index("tensor")
    z, y = dp // NY, dp % NY
    nz = n_dp // NY

    def at_z(step):
        return (lax.rem(z + step + nz, nz) * NY + y, t)

    def at_y(step):
        return (z * NY + lax.rem(y + step + NY, NY), t)

    def at_t(step):
        return (dp, lax.rem(t + step + n_t, n_t))

    return z, y, t, at_z, at_y, at_t


def greet(partners):
    barrier = pltpu.get_barrier_semaphore()
    for partner in partners:
        pl.semaphore_signal(barrier, inc=1, device_id=partner, device_id_type=MESH)
    pl.semaphore_wait(barrier, len(partners))


def remote(src, dst, send, recv, device):
    return pltpu.make_async_remote_copy(
        src_ref=src,
        dst_ref=dst,
        send_sem=send,
        recv_sem=recv,
        device_id=device,
        device_id_type=MESH,
    )


def ring_partners(nz, n_t, at_z, at_y, at_t):
    return (
        [at_t(j) for j in range(1, n_t)]
        + [at_z(1), at_z(-1)]
        + [at_y(u) for u in range(1, NY)]
    )


def gather_kernel(n_dp, n_t, m_ref, pk_ref, pv_ref, out_ref, *scratch):
    nz = n_dp // NY
    half = nz // 2
    blocks = [list(scratch[:nz]), list(scratch[nz : 2 * nz])]
    ysend, relay = scratch[2 * nz : 2 * nz + 2]
    xs, xr, xl, zs, zr, ys, yr, yl, rs, rr = scratch[2 * nz + 2 :]
    z, y, t, at_z, at_y, at_t = coordinates(n_dp, n_t)
    share = pk_ref.shape[1]
    greet(ring_partners(nz, n_t, at_z, at_y, at_t))
    sent = []

    for kv, ref in enumerate((pk_ref, pv_ref)):
        mine = pl.ds(pl.multiple_of(t * share, share), share)
        for j in range(1, n_t):
            to = at_t(j)
            cols = pl.ds(pl.multiple_of(to[1] * HD, HD), HD)
            copy = remote(
                ref.at[:, :, cols], blocks[kv][0].at[:, mine, :], xs.at[kv, j], xr.at[kv, j], to
            )
            copy.start()
            sent.append(copy)
        cols = pl.ds(pl.multiple_of(t * HD, HD), HD)
        pltpu.make_async_copy(
            ref.at[:, :, cols], blocks[kv][0].at[:, mine, :], xl.at[kv]
        ).start()

    def wait_own(kv):
        mine = pl.ds(pl.multiple_of(t * share, share), share)
        cols = pl.ds(pl.multiple_of(t * HD, HD), HD)
        ref = (pk_ref, pv_ref)[kv]
        pltpu.make_async_copy(
            ref.at[:, :, cols], blocks[kv][0].at[:, mine, :], xl.at[kv]
        ).wait()
        for j in range(1, n_t):
            src_t = lax.rem(t - j + n_t, n_t)
            rows = pl.ds(pl.multiple_of(src_t * share, share), share)
            remote(
                ref.at[:, :, cols], blocks[kv][0].at[:, rows, :], xs.at[kv, j], xr.at[kv, j], at_t(j)
            ).wait_recv()

    def push(kv, r, direction):
        nxt = (r + direction) % nz
        copy = remote(
            blocks[kv][r], blocks[kv][nxt], zs.at[kv, nxt], zr.at[kv, nxt], at_z(direction)
        )
        copy.start()
        sent.append(copy)

    def wait_block(kv, r):
        remote(
            blocks[kv][r], blocks[kv][r], zs.at[kv, r], zr.at[kv, r], at_z(1)
        ).wait_recv()

    local = []

    def spread(r):
        row = lax.rem(z - r + nz, nz)
        for u in (2, 1, 3, 0):
            to = at_y(u)
            pick = jnp.maximum(m_ref[to[0], row * NY + y], 0)
            for kv in range(2):
                ysend[r, u, kv] = blocks[kv][r][pick]
            if u == 0:
                copy = pltpu.make_async_copy(ysend.at[r, 0], out_ref.at[r * NY], yl.at[r])
                copy.start()
                local.append(copy)
            elif u == 2:
                for kv, way in enumerate((1, -1)):
                    copy = remote(
                        ysend.at[r, u, kv], relay.at[r, kv], rs.at[r, kv], rr.at[r, kv], at_y(way)
                    )
                    copy.start()
                    sent.append(copy)
            else:
                copy = remote(
                    ysend.at[r, u], out_ref.at[r * NY + u], ys.at[r, u], yr.at[r, u], to
                )
                copy.start()
                sent.append(copy)

    def forward(r):
        for kv, way in enumerate((1, -1)):
            remote(
                ysend.at[r, 2, kv], relay.at[r, kv], rs.at[r, kv], rr.at[r, kv], at_y(way)
            ).wait_recv()
            slot = 2 if kv == 0 else 0
            copy = remote(
                relay.at[r, kv], out_ref.at[r * NY + 2, kv], ys.at[r, slot], yr.at[r, slot], at_y(way)
            )
            copy.start()
            sent.append(copy)

    for kv in range(2):
        wait_own(kv)
        push(kv, 0, 1)
        push(kv, 0, -1)
    spread(0)
    waiting = [0]
    for h in range(1, half + 1):
        for kv in range(2):
            right_hops = half if kv == 0 else half - 1
            left_hops = nz - 1 - right_hops
            if h <= right_hops:
                wait_block(kv, h)
                if h < right_hops:
                    push(kv, h, 1)
            if h <= left_hops:
                wait_block(kv, nz - h)
                if h < left_hops:
                    push(kv, nz - h, -1)
        todo, waiting = waiting, [h] if h == half else [h, nz - h]
        for r in waiting:
            spread(r)
        for r in todo:
            forward(r)
    for r in waiting:
        forward(r)
    for copy in sent:
        copy.wait_send()
    for copy in local:
        copy.wait()
    for r in range(nz):
        for u in (1, 3):
            remote(
                ysend.at[r, u], out_ref.at[r * NY + u], ys.at[r, u], yr.at[r, u], at_y(u)
            ).wait_recv()
        for kv, slot in ((0, 2), (1, 0)):
            remote(
                relay.at[r, kv], out_ref.at[r * NY + 2, kv], ys.at[r, slot], yr.at[r, slot], at_y(1)
            ).wait_recv()


def gather_prompts(n_dp, n_t, table, pk, pv):
    nz = n_dp // NY
    per, share, width = pk.shape
    plen = share * n_t
    dma = pltpu.SemaphoreType.DMA
    return pl.pallas_call(
        functools.partial(gather_kernel, n_dp, n_t),
        out_shape=jax.ShapeDtypeStruct((n_dp, 2, plen, HD), BF16),
        in_specs=[
            pl.BlockSpec(memory_space=pltpu.SMEM),
            pl.BlockSpec(memory_space=pl.ANY),
            pl.BlockSpec(memory_space=pl.ANY),
        ],
        out_specs=pl.BlockSpec(memory_space=pl.ANY),
        scratch_shapes=[pltpu.VMEM((per, plen, HD), BF16) for _ in range(2 * nz)]
        + [
            pltpu.VMEM((nz, NY, 2, plen, HD), BF16),
            pltpu.VMEM((nz, 2, plen, HD), BF16),
            dma((2, n_t)),
            dma((2, n_t)),
            dma((2,)),
            dma((2, nz)),
            dma((2, nz)),
            dma((nz, NY)),
            dma((nz, NY)),
            dma((nz,)),
            dma((nz, 2)),
            dma((nz, 2)),
        ],
        compiler_params=pltpu.CompilerParams(
            collective_id=0, has_side_effects=True, vmem_limit_bytes=32 * 2**20
        ),
        name="gather_prompts",
    )(table, pk, pv)


def scatter_kernel(n_dp, n_t, m_ref, g_ref, ok_ref, ov_ref, *scratch):
    nz = n_dp // NY
    half = nz // 2
    arrived, relay, total, pieces = scratch[:4]
    chain = [[list(scratch[4 + (d * 2 + kv) * nz : 4 + (d * 2 + kv + 1) * nz]) for kv in range(2)] for d in range(2)]
    ys, yr, yl, rs, rr, zs, zr, xs, xr = scratch[4 + 4 * nz :]
    z, y, t, at_z, at_y, at_t = coordinates(n_dp, n_t)
    per, share = ok_ref.shape[:2]
    greet(ring_partners(nz, n_t, at_z, at_y, at_t))
    sent = []
    order = [half]
    for h in range(1, half):
        order += [half + h, half - h]
    order.append(0)

    def send_out(r):
        for u in (2, 1, 3):
            if u == 2:
                for kv, way in enumerate((-1, 1)):
                    copy = remote(
                        g_ref.at[r * NY + 2, kv], relay.at[r, kv], rs.at[r, kv], rr.at[r, kv], at_y(way)
                    )
                    copy.start()
                    sent.append(copy)
            else:
                copy = remote(
                    g_ref.at[r * NY + u], arrived.at[r, u], ys.at[r, u], yr.at[r, u], at_y(-u)
                )
                copy.start()
                sent.append(copy)
        pltpu.make_async_copy(g_ref.at[r * NY], arrived.at[r, 0], yl.at[r]).start()

    def forward(r):
        for kv, way in enumerate((-1, 1)):
            remote(
                g_ref.at[r * NY + 2, kv], relay.at[r, kv], rs.at[r, kv], rr.at[r, kv], at_y(way)
            ).wait_recv()
            slot = 2 if kv == 0 else 0
            copy = remote(
                relay.at[r, kv], arrived.at[r, 2, kv], ys.at[r, slot], yr.at[r, slot], at_y(way)
            )
            copy.start()
            sent.append(copy)

    def wait_y(r):
        pltpu.make_async_copy(g_ref.at[r * NY], arrived.at[r, 0], yl.at[r]).wait()
        for u in (1, 3):
            remote(
                g_ref.at[r * NY + u], arrived.at[r, u], ys.at[r, u], yr.at[r, u], at_y(-u)
            ).wait_recv()
        for kv, slot in ((0, 2), (1, 0)):
            remote(
                relay.at[r, kv], arrived.at[r, 2, kv], ys.at[r, slot], yr.at[r, slot], at_y(1)
            ).wait_recv()

    def term(r, kv, p):
        row = lax.rem(z - r + nz, nz)
        acc = None
        for u in range(NY):
            which = m_ref[at_y(u)[0], row * NY + y]
            piece = jnp.where(which == p, arrived[r, u, kv].astype(F32), 0.0)
            acc = piece if acc is None else acc + piece
        return acc

    def wait_chain(d, kv, r):
        remote(
            chain[d][kv][r], chain[d][kv][r], zs.at[d, kv, r], zr.at[d, kv, r], at_z(1)
        ).wait_recv()

    def pass_on(d, kv, r):
        step = 1 if d == 0 else -1
        nxt = (r + step) % nz
        copy = remote(
            chain[d][kv][r], chain[d][kv][nxt], zs.at[d, kv, nxt], zr.at[d, kv, nxt], at_z(step)
        )
        copy.start()
        sent.append(copy)

    def reduce_block(r):
        d = 0 if r >= half else 1
        for kv in range(2):
            way = d if r != half else kv
            first = r == half if kv == way else r == (half + 1 if way == 0 else half - 1)
            buf = chain[way][kv][r]
            if not first:
                wait_chain(way, kv, r)
            for p in range(per):
                value = term(r, kv, p)
                if not first:
                    value = value + buf[p].astype(F32)
                buf[p] = value.astype(BF16)
            pass_on(way, kv, r)

    for r in order:
        send_out(r)
    forward(order[0])
    for h in range(1, half):
        forward(half + h)
        forward(half - h)
        for r in [half] if h == 1 else [half + h - 1, half - h + 1]:
            wait_y(r)
            reduce_block(r)
    forward(0)
    for r in (nz - 1, 1):
        wait_y(r)
        reduce_block(r)
    wait_y(0)
    for kv in range(2):
        for d in range(2):
            wait_chain(d, kv, 0)
        for p in range(per):
            value = term(0, kv, p) + chain[0][kv][0][p].astype(F32) + chain[1][kv][0][p].astype(F32)
            total[kv, p] = value.astype(BF16)
        for j in range(1, n_t):
            to = at_t(j)
            rows = pl.ds(pl.multiple_of(to[1] * share, share), share)
            copy = remote(
                total.at[kv, :, rows, :], pieces.at[kv, j], xs.at[kv, j], xr.at[kv, j], to
            )
            copy.start()
            sent.append(copy)
        rows = pl.ds(pl.multiple_of(t * share, share), share)
        cols = pl.ds(pl.multiple_of(t * HD, HD), HD)
        (ok_ref, ov_ref)[kv][:, :, cols] = total[kv, :, rows, :].astype(F32)
    for kv in range(2):
        for j in range(1, n_t):
            rows = pl.ds(pl.multiple_of(t * share, share), share)
            remote(
                total.at[kv, :, rows, :], pieces.at[kv, j], xs.at[kv, j], xr.at[kv, j], at_t(j)
            ).wait_recv()
            cols = pl.ds(pl.multiple_of(at_t(-j)[1] * HD, HD), HD)
            (ok_ref, ov_ref)[kv][:, :, cols] = pieces[kv, j].astype(F32)
    for copy in sent:
        copy.wait_send()


def scatter_grads(n_dp, n_t, table, grads, per, share):
    nz = n_dp // NY
    plen = share * n_t
    dma = pltpu.SemaphoreType.DMA
    out = jax.ShapeDtypeStruct((per, share, n_t * HD), F32)
    return pl.pallas_call(
        functools.partial(scatter_kernel, n_dp, n_t),
        out_shape=(out, out),
        in_specs=[
            pl.BlockSpec(memory_space=pltpu.SMEM),
            pl.BlockSpec(memory_space=pl.ANY),
        ],
        out_specs=[pl.BlockSpec(memory_space=pltpu.VMEM)] * 2,
        scratch_shapes=[
            pltpu.VMEM((nz, NY, 2, plen, HD), BF16),
            pltpu.VMEM((nz, 2, plen, HD), BF16),
            pltpu.VMEM((2, per, plen, HD), BF16),
            pltpu.VMEM((2, n_t, per, share, HD), BF16),
        ]
        + [pltpu.VMEM((per, plen, HD), BF16) for _ in range(4 * nz)]
        + [
            dma((nz, NY)),
            dma((nz, NY)),
            dma((nz,)),
            dma((nz, 2)),
            dma((nz, 2)),
            dma((2, 2, nz)),
            dma((2, 2, nz)),
            dma((2, n_t)),
            dma((2, n_t)),
        ],
        compiler_params=pltpu.CompilerParams(
            collective_id=1, has_side_effects=True, vmem_limit_bytes=32 * 2**20
        ),
        name="scatter_grads",
    )(table, grads)


def dot(a, b, dims):
    return lax.dot_general(a, b, (dims, ((), ())), preferred_element_type=F32)


def attend_slot(length, queries, cotangent, keys, values, heads):
    rows = queries.shape[0]
    count = keys.shape[0]
    tokens = rows // heads
    prefix = count - tokens
    scale = 1.0 / math.sqrt(HD)
    token = lax.rem(lax.broadcasted_iota(jnp.int32, (1, rows), 1), tokens)
    valid = lax.rem(lax.broadcasted_iota(jnp.int32, (rows, 1), 0), tokens) < length
    cotangent = jnp.where(valid, cotangent, jnp.zeros_like(cotangent))
    scores = dot(keys, queries, ((1,), (1,)))
    dweights = dot(values, cotangent, ((1,), (1,)))
    key = lax.broadcasted_iota(jnp.int32, (tokens, rows), 0)
    tail = jnp.where(key <= token, scores[prefix:], NEG)
    scores = jnp.concatenate([scores[:prefix], tail], axis=0)
    top = jnp.max(scores, axis=0, keepdims=True)
    exponent = jnp.exp2((scores - top) * (scale * math.log2(math.e)))
    probs = exponent * (1.0 / jnp.sum(exponent, axis=0, keepdims=True))
    weights = probs.astype(BF16)
    delta = jnp.sum(probs * dweights, axis=0, keepdims=True)
    dscores = (probs * (dweights - delta) * scale).astype(BF16)
    out = dot(weights, values, ((0,), (0,)))
    out = jnp.where(valid, out, 0.0).astype(BF16)
    dq = dot(dscores, keys, ((0,), (0,))).astype(BF16)
    dk = dot(dscores, queries, ((1,), (0,)))
    dv = dot(weights, cotangent, ((1,), (0,)))
    return out, dq, dk, dv


def attend_kernel(
    batch, index_ref, len_ref, q_ref, do_ref, ck_ref, cv_ref, pre_ref, out_ref, dq_ref, dk_ref, dv_ref, g_ref
):
    step = pl.program_id(0)
    heads = q_ref.shape[2] // HD
    tokens = q_ref.shape[1]
    prefix = pre_ref.shape[2]
    for b in range(batch):
        s = step * batch + b
        place = index_ref[s]
        queries = jnp.concatenate([q_ref[b, :, h * HD : (h + 1) * HD] for h in range(heads)], axis=0)
        cotangent = jnp.concatenate([do_ref[b, :, h * HD : (h + 1) * HD] for h in range(heads)], axis=0)
        keys = jnp.concatenate([pre_ref[place, 0], ck_ref[b]], axis=0)
        values = jnp.concatenate([pre_ref[place, 1], cv_ref[b]], axis=0)
        out, dq, dk, dv = attend_slot(len_ref[s], queries, cotangent, keys, values, heads)
        for h in range(heads):
            out_ref[b, :, h * HD : (h + 1) * HD] = out[h * tokens : (h + 1) * tokens]
            dq_ref[b, :, h * HD : (h + 1) * HD] = dq[h * tokens : (h + 1) * tokens]
        dk_ref[b] = dk[prefix:].astype(BF16)
        dv_ref[b] = dv[prefix:].astype(BF16)
        g_ref[place, 0] = dk[:prefix].astype(BF16)
        g_ref[place, 1] = dv[:prefix].astype(BF16)


def attend(index, cont_len, q, do, ck, cv, pre, batch=2):
    slots, tokens, width = q.shape
    wide = pl.BlockSpec((batch, tokens, width), lambda i, *_: (i, 0, 0))
    thin = pl.BlockSpec((batch, tokens, HD), lambda i, *_: (i, 0, 0))
    whole = pl.BlockSpec(pre.shape, lambda i, *_: (0, 0, 0, 0))
    flops = 12 * slots * tokens * (tokens + pre.shape[2]) * width
    return pl.pallas_call(
        functools.partial(attend_kernel, batch),
        grid_spec=pltpu.PrefetchScalarGridSpec(
            num_scalar_prefetch=2,
            grid=(slots // batch,),
            in_specs=[wide, wide, thin, thin, whole],
            out_specs=[wide, wide, thin, thin, whole],
        ),
        out_shape=(
            jax.ShapeDtypeStruct(q.shape, BF16),
            jax.ShapeDtypeStruct(q.shape, BF16),
            jax.ShapeDtypeStruct(ck.shape, BF16),
            jax.ShapeDtypeStruct(cv.shape, BF16),
            jax.ShapeDtypeStruct(pre.shape, BF16),
        ),
        compiler_params=pltpu.CompilerParams(vmem_limit_bytes=40 * 2**20),
        cost_estimate=pl.CostEstimate(flops=flops, bytes_accessed=4 * q.size * 2, transcendentals=q.size),
        name="attend",
    )(index, cont_len, q, do, ck, cv, pre)


def on_device(n_dp, n_t, cont_q, cont_k, cont_v, out_grad, prompt_k, prompt_v, cont_len, cont_prompt):
    slots = cont_q.shape[0]
    per, share = prompt_k.shape[:2]
    nz = n_dp // NY
    dp = lax.axis_index("dp")
    named = cont_prompt.reshape(n_dp, slots, 1)
    owner = lax.broadcasted_iota(jnp.int32, (1, 1, n_dp), 2)
    table = jnp.max(jnp.where(named // per == owner, named % per, -1), axis=1)
    mine = lax.dynamic_slice_in_dim(cont_prompt, dp * slots, slots) // per
    index = ((dp // NY - mine // NY + nz) % nz) * NY + (dp % NY - mine % NY + NY) % NY
    pre = gather_prompts(n_dp, n_t, table, prompt_k, prompt_v)
    out, dq, dk, dv, grads = attend(index, cont_len, cont_q, out_grad, cont_k, cont_v, pre)
    gk, gv = scatter_grads(n_dp, n_t, table, grads, per, share)
    return out, dq, dk, dv, gk, gv


def solution(mesh):
    n_dp, n_t = mesh.shape["dp"], mesh.shape["tensor"]
    return jax.shard_map(
        functools.partial(on_device, n_dp, n_t),
        mesh=mesh,
        in_specs=(
            P("dp", None, "tensor"),
            P("dp", None, "tensor"),
            P("dp", None, "tensor"),
            P("dp", None, "tensor"),
            P("dp", "tensor", None),
            P("dp", "tensor", None),
            P("dp"),
            P(),
        ),
        out_specs=(
            P("dp", None, "tensor"),
            P("dp", None, "tensor"),
            P("dp", None, "tensor"),
            P("dp", None, "tensor"),
            P("dp", "tensor", None),
            P("dp", "tensor", None),
        ),
        check_vma=False,
    )
```

```python
import functools
import math

import jax
import jax.numpy as jnp
from jax import lax
from jax.experimental import pallas as pl
from jax.experimental.pallas import tpu as pltpu
from jax.sharding import PartitionSpec as P

HD = 128
NY = 4
NEG = -1e30
VMEM_LIMIT = 56 * 2**20
MESH = pl.DeviceIdType.MESH
BF16 = jnp.bfloat16
F32 = jnp.float32


def coordinates(n_dp, n_t):
    dp = lax.axis_index("dp")
    t = lax.axis_index("tensor")
    z, y = dp // NY, dp % NY
    nz = n_dp // NY

    def at_z(step):
        return (lax.rem(z + step + nz, nz) * NY + y, t)

    def at_y(step):
        return (z * NY + lax.rem(y + step + NY, NY), t)

    def at_t(step):
        return (dp, lax.rem(t + step + n_t, n_t))

    def at_zy(step, u):
        return (lax.rem(z + step + nz, nz) * NY + lax.rem(y + u + NY, NY), t)

    return z, y, t, at_z, at_y, at_t, at_zy


def greet(devices):
    barrier = pltpu.get_barrier_semaphore()
    for device in devices:
        pl.semaphore_signal(barrier, inc=1, device_id=device, device_id_type=MESH)
    pl.semaphore_wait(barrier, len(devices))


def remote(src, dst, send, recv, device):
    return pltpu.make_async_remote_copy(
        src_ref=src,
        dst_ref=dst,
        send_sem=send,
        recv_sem=recv,
        device_id=device,
        device_id_type=MESH,
    )


def partners(n_t, at_z, at_y, at_t, at_zy):
    return (
        [at_t(j) for j in range(1, n_t)]
        + [at_y(u) for u in range(1, NY)]
        + [at_zy(way, u) for way in (1, -1) for u in range(NY)]
    )


def gather_kernel(n_dp, n_t, m_ref, pk_ref, pv_ref, out_ref, *scratch):
    nz = n_dp // NY
    half = nz // 2
    blocks = [list(scratch[:nz]), list(scratch[nz : 2 * nz])]
    picked, xs, xr, xl, zs, zr, ys, yr, yl = scratch[2 * nz :]
    z, y, t, at_z, at_y, at_t, at_zy = coordinates(n_dp, n_t)
    share = pk_ref.shape[1]
    greet(partners(n_t, at_z, at_y, at_t, at_zy))
    sent = []

    def start(*args):
        copy = remote(*args)
        copy.start()
        sent.append(copy)

    mine = pl.ds(pl.multiple_of(t * share, share), share)
    own = pl.ds(pl.multiple_of(t * HD, HD), HD)
    local = []
    for kv, ref in enumerate((pk_ref, pv_ref)):
        for j in range(1, n_t):
            to = at_t(j)
            cols = pl.ds(pl.multiple_of(to[1] * HD, HD), HD)
            start(ref.at[:, :, cols], blocks[kv][0].at[:, mine, :], xs.at[kv, j], xr.at[kv, j], to)
        local.append(pltpu.make_async_copy(ref.at[:, :, own], blocks[kv][0].at[:, mine, :], xl.at[kv]))
        local[kv].start()

    def wait_own(kv):
        local[kv].wait()
        for j in range(1, n_t):
            rows = pl.ds(pl.multiple_of(at_t(-j)[1] * share, share), share)
            remote(
                (pk_ref, pv_ref)[kv].at[:, :, own], blocks[kv][0].at[:, rows, :], xs.at[kv, j], xr.at[kv, j], at_t(j)
            ).wait_recv()

    def push(kv, r, way):
        nxt = (r + way) % nz
        start(blocks[kv][r], blocks[kv][nxt], zs.at[kv, nxt], zr.at[kv, nxt], at_z(way))

    def wait_block(kv, r):
        remote(blocks[kv][r], blocks[kv][r], zs.at[kv, r], zr.at[kv, r], at_z(1)).wait_recv()

    def spread(kv, r, way):
        row = lax.rem(z - r + nz, nz)
        there = (r + way) % nz
        for u in (2, 1, 3, 0):
            to = at_zy(way, u)
            pick = jnp.maximum(m_ref[to[0], row * NY + y], 0)
            picked[there, u, kv] = blocks[kv][r][pick]
            place = out_ref.at[there * NY + u, kv]
            if u == 0 and way == 0:
                copy = pltpu.make_async_copy(picked.at[there, u, kv], place, yl.at[there, kv])
                copy.start()
                local.append(copy)
            else:
                start(picked.at[there, u, kv], place, ys.at[there, u, kv], yr.at[there, u, kv], to)

    for kv in range(2):
        wait_own(kv)
        push(kv, 0, 1)
        push(kv, 0, -1)
    for kv in range(2):
        spread(kv, 0, 0)
    for h in range(1, half):
        for kv in range(2):
            for r, way in ((h, 1), (nz - h, -1)):
                wait_block(kv, r)
                if h < half - 1:
                    push(kv, r, way)
                elif kv == (0 if way == 1 else 1):
                    spread(kv, r, way)
        for kv in range(2):
            for r in (h, nz - h):
                spread(kv, r, 0)
    for copy in local[2:]:
        copy.wait()
    for copy in sent:
        copy.wait_send()
    for r in range(nz):
        for u in range(NY):
            for kv in range(2):
                if u or r == half:
                    place = out_ref.at[r * NY + u, kv]
                    remote(
                        picked.at[r, u, kv], place, ys.at[r, u, kv], yr.at[r, u, kv], at_y(1)
                    ).wait_recv()


def gather_prompts(n_dp, n_t, table, pk, pv, cid=0):
    nz = n_dp // NY
    per, share, width = pk.shape
    plen = share * n_t
    dma = pltpu.SemaphoreType.DMA
    return pl.pallas_call(
        functools.partial(gather_kernel, n_dp, n_t),
        out_shape=jax.ShapeDtypeStruct((n_dp, 2, plen, HD), BF16),
        in_specs=[
            pl.BlockSpec(memory_space=pltpu.SMEM),
            pl.BlockSpec(memory_space=pl.ANY),
            pl.BlockSpec(memory_space=pl.ANY),
        ],
        out_specs=pl.BlockSpec(memory_space=pl.ANY),
        scratch_shapes=[pltpu.VMEM((per, plen, HD), BF16) for _ in range(2 * nz)]
        + [
            pltpu.VMEM((nz, NY, 2, plen, HD), BF16),
            dma((2, n_t)),
            dma((2, n_t)),
            dma((2,)),
            dma((2, nz)),
            dma((2, nz)),
            dma((nz, NY, 2)),
            dma((nz, NY, 2)),
            dma((nz, 2)),
        ],
        compiler_params=pltpu.CompilerParams(
            collective_id=cid, has_side_effects=True, vmem_limit_bytes=VMEM_LIMIT
        ),
        name="gather_prompts",
    )(table, pk, pv)


def scatter_kernel(n_dp, n_t, m_ref, g_ref, ok_ref, ov_ref, *scratch):
    nz = n_dp // NY
    half = nz // 2
    arrived, far, chain, total, pieces, ys, yr, yl, fs, fr, zs, zr, xs, xr = scratch
    z, y, t, at_z, at_y, at_t, at_zy = coordinates(n_dp, n_t)
    per, share = ok_ref.shape[:2]
    greet(partners(n_t, at_z, at_y, at_t, at_zy))
    sent = []

    def start(*args):
        copy = remote(*args)
        copy.start()
        sent.append(copy)

    def send_far(kv):
        for u in range(NY):
            src = g_ref.at[half * NY + u, kv]
            start(src, far.at[kv, u], fs.at[kv, u], fr.at[kv, u], at_zy(-1 if kv == 0 else 1, -u))

    def wait_far(kv):
        for u in range(NY):
            src = g_ref.at[half * NY + u, kv]
            remote(src, far.at[kv, u], fs.at[kv, u], fr.at[kv, u], at_y(1)).wait_recv()

    def send_out(kv, r):
        for u in (2, 1, 3):
            start(g_ref.at[r * NY + u, kv], arrived.at[r, u, kv], ys.at[r, u, kv], yr.at[r, u, kv], at_y(-u))
        pltpu.make_async_copy(g_ref.at[r * NY, kv], arrived.at[r, 0, kv], yl.at[r, kv]).start()

    def wait_y(kv, r):
        pltpu.make_async_copy(g_ref.at[r * NY, kv], arrived.at[r, 0, kv], yl.at[r, kv]).wait()
        for u in range(1, NY):
            remote(
                g_ref.at[r * NY + u, kv], arrived.at[r, u, kv], ys.at[r, u, kv], yr.at[r, u, kv], at_y(1)
            ).wait_recv()

    def sums(kv, r, store, *more):
        row = lax.rem(z - r + nz, nz)
        column = row * NY + y
        parts = [(m_ref[at_y(u)[0], column], arrived.at[r, u, kv]) for u in range(NY)]
        if r == (half - 1 if kv == 0 else half + 1):
            way = 1 if kv == 0 else -1
            parts += [(m_ref[at_zy(way, u)[0], column], far.at[kv, u]) for u in range(NY)]
        for p in range(per):
            acc = None
            for which, ref in parts:
                piece = jnp.where(which == p, ref[...].astype(F32), 0.0)
                acc = piece if acc is None else acc + piece
            for ref in more:
                acc = acc + ref[p].astype(F32)
            store[p] = acc.astype(BF16)

    def wait_chain(d, kv, r):
        remote(
            chain.at[d, kv, r], chain.at[d, kv, r], zs.at[d, kv, r], zr.at[d, kv, r], at_z(1)
        ).wait_recv()

    def reduce_block(kv, r):
        d = 0 if r > half else 1
        buf = chain.at[d, kv, r]
        if r in (half - 1, half + 1):
            sums(kv, r, buf)
        else:
            wait_chain(d, kv, r)
            sums(kv, r, buf, buf)
        step = 1 if d == 0 else -1
        nxt = (r + step) % nz
        start(buf, chain.at[d, kv, nxt], zs.at[d, kv, nxt], zr.at[d, kv, nxt], at_z(step))

    for kv in range(2):
        send_far(kv)
        for r in (half - 1, half + 1):
            send_out(kv, r)
    for h in range(half - 1, 0, -1):
        for kv in range(2):
            for r in (h, nz - h):
                wait_y(kv, r)
            for r in (h - 1, nz - h + 1) if h > 1 else (0,):
                send_out(kv, r)
            if h == half - 1:
                wait_far(kv)
            for r in (h, nz - h):
                reduce_block(kv, r)
    mine = pl.ds(pl.multiple_of(t * share, share), share)
    own = pl.ds(pl.multiple_of(t * HD, HD), HD)
    for kv in range(2):
        wait_y(kv, 0)
        for d in range(2):
            wait_chain(d, kv, 0)
        sums(kv, 0, total.at[kv], chain.at[0, kv, 0], chain.at[1, kv, 0])
        for j in range(1, n_t):
            to = at_t(j)
            rows = pl.ds(pl.multiple_of(to[1] * share, share), share)
            start(total.at[kv, :, rows, :], pieces.at[kv, j], xs.at[kv, j], xr.at[kv, j], to)
        (ok_ref, ov_ref)[kv][:, :, own] = total[kv, :, mine, :].astype(F32)
    for kv in range(2):
        for j in range(1, n_t):
            remote(
                total.at[kv, :, mine, :], pieces.at[kv, j], xs.at[kv, j], xr.at[kv, j], at_t(j)
            ).wait_recv()
            cols = pl.ds(pl.multiple_of(at_t(-j)[1] * HD, HD), HD)
            (ok_ref, ov_ref)[kv][:, :, cols] = pieces[kv, j].astype(F32)
    for copy in sent:
        copy.wait_send()


def scatter_grads(n_dp, n_t, table, grads, per, share, cid=1):
    nz = n_dp // NY
    plen = share * n_t
    dma = pltpu.SemaphoreType.DMA
    out = jax.ShapeDtypeStruct((per, share, n_t * HD), F32)
    return pl.pallas_call(
        functools.partial(scatter_kernel, n_dp, n_t),
        out_shape=(out, out),
        in_specs=[
            pl.BlockSpec(memory_space=pltpu.SMEM),
            pl.BlockSpec(memory_space=pl.ANY),
        ],
        out_specs=[pl.BlockSpec(memory_space=pltpu.VMEM)] * 2,
        scratch_shapes=[
            pltpu.VMEM((nz, NY, 2, plen, HD), BF16),
            pltpu.VMEM((2, NY, plen, HD), BF16),
            pltpu.VMEM((2, 2, nz, per, plen, HD), BF16),
            pltpu.VMEM((2, per, plen, HD), BF16),
            pltpu.VMEM((2, n_t, per, share, HD), BF16),
            dma((nz, NY, 2)),
            dma((nz, NY, 2)),
            dma((nz, 2)),
            dma((2, NY)),
            dma((2, NY)),
            dma((2, 2, nz)),
            dma((2, 2, nz)),
            dma((2, n_t)),
            dma((2, n_t)),
        ],
        compiler_params=pltpu.CompilerParams(
            collective_id=cid, has_side_effects=True, vmem_limit_bytes=VMEM_LIMIT
        ),
        name="scatter_grads",
    )(table, grads)


def dot(a, b, dims):
    return lax.dot_general(a, b, (dims, ((), ())), preferred_element_type=F32)


def attend_slot(length, queries, cotangent, keys, values, heads):
    rows = queries.shape[0]
    count = keys.shape[0]
    tokens = rows // heads
    prefix = count - tokens
    scale = 1.0 / math.sqrt(HD)
    token = lax.rem(lax.broadcasted_iota(jnp.int32, (1, rows), 1), tokens)
    valid = lax.rem(lax.broadcasted_iota(jnp.int32, (rows, 1), 0), tokens) < length
    cotangent = jnp.where(valid, cotangent, jnp.zeros_like(cotangent))
    scores = dot(keys, queries, ((1,), (1,)))
    dweights = dot(values, cotangent, ((1,), (1,)))
    key = lax.broadcasted_iota(jnp.int32, (tokens, rows), 0)
    tail = jnp.where(key <= token, scores[prefix:], NEG)
    scores = jnp.concatenate([scores[:prefix], tail], axis=0)
    top = jnp.max(scores, axis=0, keepdims=True)
    exponent = jnp.exp2((scores - top) * (scale * math.log2(math.e)))
    probs = exponent * (1.0 / jnp.sum(exponent, axis=0, keepdims=True))
    weights = probs.astype(BF16)
    delta = jnp.sum(probs * dweights, axis=0, keepdims=True)
    dscores = (probs * (dweights - delta) * scale).astype(BF16)
    out = dot(weights, values, ((0,), (0,)))
    out = jnp.where(valid, out, 0.0).astype(BF16)
    dq = dot(dscores, keys, ((0,), (0,))).astype(BF16)
    dk = dot(dscores, queries, ((1,), (0,)))
    dv = dot(weights, cotangent, ((1,), (0,)))
    return out, dq, dk, dv


def attend_kernel(
    batch, per, named_ref, len_ref, q_ref, do_ref, ck_ref, cv_ref, pre_ref, out_ref, dq_ref, dk_ref, dv_ref, g_ref
):
    step = pl.program_id(0)
    dp = lax.axis_index("dp")
    slots = len_ref.shape[0]
    nz = pre_ref.shape[0] // NY
    heads = q_ref.shape[2] // HD
    tokens = q_ref.shape[1]
    prefix = pre_ref.shape[2]
    for b in range(batch):
        s = step * batch + b
        owner = named_ref[dp * slots + s] // per
        row = lax.rem(dp // NY - owner // NY + nz, nz)
        place = row * NY + lax.rem(dp % NY - owner % NY + NY, NY)
        queries = jnp.concatenate([q_ref[b, :, h * HD : (h + 1) * HD] for h in range(heads)], axis=0)
        cotangent = jnp.concatenate([do_ref[b, :, h * HD : (h + 1) * HD] for h in range(heads)], axis=0)
        keys = jnp.concatenate([pre_ref[place, 0], ck_ref[b]], axis=0)
        values = jnp.concatenate([pre_ref[place, 1], cv_ref[b]], axis=0)
        out, dq, dk, dv = attend_slot(len_ref[s], queries, cotangent, keys, values, heads)
        for h in range(heads):
            out_ref[b, :, h * HD : (h + 1) * HD] = out[h * tokens : (h + 1) * tokens]
            dq_ref[b, :, h * HD : (h + 1) * HD] = dq[h * tokens : (h + 1) * tokens]
        dk_ref[b] = dk[prefix:].astype(BF16)
        dv_ref[b] = dv[prefix:].astype(BF16)
        g_ref[place, 0] = dk[:prefix].astype(BF16)
        g_ref[place, 1] = dv[:prefix].astype(BF16)


def attend(per, named, cont_len, q, do, ck, cv, pre, batch=2):
    slots, tokens, width = q.shape
    wide = pl.BlockSpec((batch, tokens, width), lambda i, *_: (i, 0, 0))
    thin = pl.BlockSpec((batch, tokens, HD), lambda i, *_: (i, 0, 0))
    whole = pl.BlockSpec(pre.shape, lambda i, *_: (0, 0, 0, 0))
    flops = 12 * slots * tokens * (tokens + pre.shape[2]) * width
    return pl.pallas_call(
        functools.partial(attend_kernel, batch, per),
        grid_spec=pltpu.PrefetchScalarGridSpec(
            num_scalar_prefetch=2,
            grid=(slots // batch,),
            in_specs=[wide, wide, thin, thin, whole],
            out_specs=[wide, wide, thin, thin, whole],
        ),
        out_shape=(
            jax.ShapeDtypeStruct(q.shape, BF16),
            jax.ShapeDtypeStruct(q.shape, BF16),
            jax.ShapeDtypeStruct(ck.shape, BF16),
            jax.ShapeDtypeStruct(cv.shape, BF16),
            jax.ShapeDtypeStruct(pre.shape, BF16),
        ),
        compiler_params=pltpu.CompilerParams(vmem_limit_bytes=VMEM_LIMIT),
        cost_estimate=pl.CostEstimate(flops=flops, bytes_accessed=4 * q.size * 2, transcendentals=q.size),
        name="attend",
    )(named, cont_len, q, do, ck, cv, pre)


def on_device(n_dp, n_t, cont_q, cont_k, cont_v, out_grad, prompt_k, prompt_v, cont_len, cont_prompt):
    slots = cont_q.shape[0]
    per, share = prompt_k.shape[:2]
    owner = lax.broadcasted_iota(jnp.int32, (1, 1, n_dp), 2)
    offset = cont_prompt.reshape(n_dp, slots, 1) - owner * per
    table = jnp.max(jnp.where((offset >= 0) & (offset < per), offset, -1), axis=1)
    pre = gather_prompts(n_dp, n_t, table, prompt_k, prompt_v)
    out, dq, dk, dv, grads = attend(per, cont_prompt, cont_len, cont_q, out_grad, cont_k, cont_v, pre)
    gk, gv = scatter_grads(n_dp, n_t, table, grads, per, share)
    return out, dq, dk, dv, gk, gv


def solution(mesh):
    n_dp, n_t = mesh.shape["dp"], mesh.shape["tensor"]
    return jax.shard_map(
        functools.partial(on_device, n_dp, n_t),
        mesh=mesh,
        in_specs=(
            P("dp", None, "tensor"),
            P("dp", None, "tensor"),
            P("dp", None, "tensor"),
            P("dp", None, "tensor"),
            P("dp", "tensor", None),
            P("dp", "tensor", None),
            P("dp"),
            P(),
        ),
        out_specs=(
            P("dp", None, "tensor"),
            P("dp", None, "tensor"),
            P("dp", None, "tensor"),
            P("dp", None, "tensor"),
            P("dp", "tensor", None),
            P("dp", "tensor", None),
        ),
        check_vma=False,
    )
```

```python
import functools
import math

import jax
import jax.numpy as jnp
from jax import lax
from jax.experimental import pallas as pl
from jax.experimental.pallas import tpu as pltpu
from jax.sharding import PartitionSpec as P

HD = 128
NY = 4
PACK = 8
NEG = -1e30
VMEM_LIMIT = 56 * 2**20
FINISH_LIMIT = 56 * 2**20
MESH = pl.DeviceIdType.MESH
BF16 = jnp.bfloat16
F32 = jnp.float32


def coordinates(n_dp, n_t):
    dp = lax.axis_index("dp")
    t = lax.axis_index("tensor")
    z, y = dp // NY, dp % NY
    nz = n_dp // NY

    def at_z(step):
        return (lax.rem(z + step + nz, nz) * NY + y, t)

    def at_y(step):
        return (z * NY + lax.rem(y + step + NY, NY), t)

    def at_t(step):
        return (dp, lax.rem(t + step + n_t, n_t))

    def at_zy(step, u):
        return (lax.rem(z + step + nz, nz) * NY + lax.rem(y + u + NY, NY), t)

    return z, y, t, at_z, at_y, at_t, at_zy


def greet(devices):
    barrier = pltpu.get_barrier_semaphore()
    for device in devices:
        pl.semaphore_signal(barrier, inc=1, device_id=device, device_id_type=MESH)
    pl.semaphore_wait(barrier, len(devices))


def remote(src, dst, send, recv, device):
    return pltpu.make_async_remote_copy(
        src_ref=src,
        dst_ref=dst,
        send_sem=send,
        recv_sem=recv,
        device_id=device,
        device_id_type=MESH,
    )


def partners(n_t, at_z, at_y, at_t, at_zy):
    return (
        [at_t(j) for j in range(1, n_t)]
        + [at_y(u) for u in range(1, NY)]
        + [at_zy(way, u) for way in (1, -1) for u in range(NY)]
    )


def gather_kernel(n_dp, n_t, m_ref, pk_ref, pv_ref, out_ref, *scratch):
    nz = n_dp // NY
    half = nz // 2
    blocks = [list(scratch[:nz]), list(scratch[nz : 2 * nz])]
    picked, xs, xr, xl, zs, zr, ys, yr, yl = scratch[2 * nz :]
    z, y, t, at_z, at_y, at_t, at_zy = coordinates(n_dp, n_t)
    share = pk_ref.shape[1]
    greet(partners(n_t, at_z, at_y, at_t, at_zy))
    sent = []

    def start(*args):
        copy = remote(*args)
        copy.start()
        sent.append(copy)

    mine = pl.ds(pl.multiple_of(t * share, share), share)
    own = pl.ds(pl.multiple_of(t * HD, HD), HD)
    local = []
    for kv, ref in enumerate((pk_ref, pv_ref)):
        for copy in sent:
            copy.wait_send()
        sent.clear()
        for j in range(1, n_t):
            to = at_t(j)
            cols = pl.ds(pl.multiple_of(to[1] * HD, HD), HD)
            start(ref.at[:, :, cols], blocks[kv][0].at[:, mine, :], xs.at[kv, j], xr.at[kv, j], to)
        local.append(pltpu.make_async_copy(ref.at[:, :, own], blocks[kv][0].at[:, mine, :], xl.at[kv]))
        local[kv].start()

    def wait_own(kv):
        local[kv].wait()
        for j in range(1, n_t):
            rows = pl.ds(pl.multiple_of(at_t(-j)[1] * share, share), share)
            remote(
                (pk_ref, pv_ref)[kv].at[:, :, own], blocks[kv][0].at[:, rows, :], xs.at[kv, j], xr.at[kv, j], at_t(j)
            ).wait_recv()

    def push(kv, r, way):
        nxt = (r + way) % nz
        start(blocks[kv][r], blocks[kv][nxt], zs.at[kv, nxt], zr.at[kv, nxt], at_z(way))

    def wait_block(kv, r):
        remote(blocks[kv][r], blocks[kv][r], zs.at[kv, r], zr.at[kv, r], at_z(1)).wait_recv()

    def spread(kv, r, way):
        row = lax.rem(z - r + nz, nz)
        there = (r + way) % nz
        for u in (2, 1, 3, 0):
            to = at_zy(way, u)
            pick = lax.rem(jnp.maximum(m_ref[to[0], row * NY + y], 0), PACK)
            picked[there, u, kv] = blocks[kv][r][pick]
            place = out_ref.at[there * NY + u, kv]
            if u == 0 and way == 0:
                copy = pltpu.make_async_copy(picked.at[there, u, kv], place, yl.at[there, kv])
                copy.start()
                local.append(copy)
            else:
                start(picked.at[there, u, kv], place, ys.at[there, u, kv], yr.at[there, u, kv], to)

    for kv in range(2):
        wait_own(kv)
        push(kv, 0, 1)
        push(kv, 0, -1)
    for kv in range(2):
        spread(kv, 0, 0)
    for h in range(1, half):
        for kv in range(2):
            for r, way in ((h, 1), (nz - h, -1)):
                wait_block(kv, r)
                if h < half - 1:
                    push(kv, r, way)
                elif kv == (0 if way == 1 else 1):
                    spread(kv, r, way)
            for r in (h, nz - h):
                spread(kv, r, 0)
    for copy in local[2:]:
        copy.wait()
    for copy in sent:
        copy.wait_send()
    for r in range(nz):
        for u in range(NY):
            for kv in range(2):
                if u or r == half:
                    place = out_ref.at[r * NY + u, kv]
                    remote(
                        picked.at[r, u, kv], place, ys.at[r, u, kv], yr.at[r, u, kv], at_y(1)
                    ).wait_recv()


def gather_prompts(n_dp, n_t, table, pk, pv, cid=0):
    nz = n_dp // NY
    per, share, width = pk.shape
    plen = share * n_t
    dma = pltpu.SemaphoreType.DMA
    return pl.pallas_call(
        functools.partial(gather_kernel, n_dp, n_t),
        out_shape=jax.ShapeDtypeStruct((n_dp, 2, plen, HD), BF16),
        in_specs=[
            pl.BlockSpec(memory_space=pltpu.SMEM),
            pl.BlockSpec(memory_space=pl.ANY),
            pl.BlockSpec(memory_space=pl.ANY),
        ],
        out_specs=pl.BlockSpec(memory_space=pl.ANY),
        scratch_shapes=[pltpu.VMEM((per, plen, HD), BF16) for _ in range(2 * nz)]
        + [
            pltpu.VMEM((nz, NY, 2, plen, HD), BF16),
            dma((2, n_t)),
            dma((2, n_t)),
            dma((2,)),
            dma((2, nz)),
            dma((2, nz)),
            dma((nz, NY, 2)),
            dma((nz, NY, 2)),
            dma((nz, 2)),
        ],
        compiler_params=pltpu.CompilerParams(
            collective_id=cid, has_side_effects=True, vmem_limit_bytes=VMEM_LIMIT
        ),
        name="gather_prompts",
    )(table, pk, pv)


def attend_scatter_kernel(
    n_dp, n_t, m_ref, len_ref, q_ref, do_ref, ck_ref, cv_ref, pre_ref, out_ref, dq_ref, tail_ref, ok_ref, ov_ref, *scratch
):
    nz = n_dp // NY
    half = nz // 2
    qb, dob, ckb, cvb, preb, ob, dqb, tailb, g_ref = scratch[:9]
    arrived, far, chain, term, total, pieces, ins, pres, outs, ys, yr, yl, fs, fr, zs, zr, xs, xr = scratch[9:]
    z, y, t, at_z, at_y, at_t, at_zy = coordinates(n_dp, n_t)
    per, share = ok_ref.shape[:2]
    dp = z * NY + y
    slots, tokens, width = q_ref.shape
    heads = width // HD
    prefix = pre_ref.shape[2]
    local = [
        pltpu.make_async_copy(src, dst, ins.at[i])
        for i, (src, dst) in enumerate(((q_ref, qb), (do_ref, dob), (ck_ref, ckb), (cv_ref, cvb)))
    ]

    def prompts(r):
        return pltpu.make_async_copy(pre_ref.at[pl.ds(r * NY, NY)], preb.at[pl.ds(r * NY, NY)], pres.at[r])

    def results(r):
        part = pl.ds(r * NY, NY)
        return [
            pltpu.make_async_copy(src.at[part], dst.at[part], outs.at[i, r])
            for i, (src, dst) in enumerate(((ob, out_ref), (dqb, dq_ref), (tailb, tail_ref)))
        ]

    for copy in local:
        copy.start()
    order = [half]
    for h in range(half - 1, 0, -1):
        order += [h, nz - h]
    order.append(0)
    for r in order:
        prompts(r).start()
    greet(partners(n_t, at_z, at_y, at_t, at_zy))

    def far_copy(kv, u):
        src = g_ref.at[half * NY + u, kv]
        return remote(src, far.at[kv, u], fs.at[kv, u], fr.at[kv, u], at_zy(-1 if kv == 0 else 1, -u))

    def out_copy(kv, r, u):
        return remote(
            g_ref.at[r * NY + u, kv], arrived.at[r, u, kv], ys.at[r, u, kv], yr.at[r, u, kv], at_y(-u)
        )

    def chain_copy(kv, r):
        d = 0 if r > half else 1
        step = 1 if d == 0 else -1
        nxt = (r + step) % nz
        return remote(
            chain.at[d, kv, r], chain.at[d, kv, nxt], zs.at[d, kv, nxt], zr.at[d, kv, nxt], at_z(step)
        )

    def piece_copy(kv, j):
        to = at_t(j)
        rows = pl.ds(pl.multiple_of(to[1] * share, share), share)
        return remote(total.at[kv, :, rows, :], pieces.at[kv, j], xs.at[kv, j], xr.at[kv, j], to)

    def send_out(kv, r):
        for u in (2, 1, 3):
            out_copy(kv, r, u).start()
        pltpu.make_async_copy(g_ref.at[r * NY, kv], arrived.at[r, 0, kv], yl.at[r, kv]).start()

    def wait_y(kv, r):
        pltpu.make_async_copy(g_ref.at[r * NY, kv], arrived.at[r, 0, kv], yl.at[r, kv]).wait()
        for u in range(1, NY):
            out_copy(kv, r, u).wait_recv()

    def sums(kv, r, store):
        row = lax.rem(z - r + nz, nz)
        column = row * NY + y
        parts = [(lax.rem(m_ref[at_y(u)[0], column], PACK), arrived.at[r, u, kv]) for u in range(NY)]
        if r == (half - 1 if kv == 0 else half + 1):
            way = 1 if kv == 0 else -1
            parts += [(lax.rem(m_ref[at_zy(way, u)[0], column], PACK), far.at[kv, u]) for u in range(NY)]
        for p in range(per):
            acc = None
            for which, ref in parts:
                piece = jnp.where(which == p, ref[...].astype(F32), 0.0)
                acc = piece if acc is None else acc + piece
            store[p] = acc.astype(store.dtype)

    def wait_chain(d, kv, r):
        remote(
            chain.at[d, kv, r], chain.at[d, kv, r], zs.at[d, kv, r], zr.at[d, kv, r], at_z(1)
        ).wait_recv()

    def reduce_block(kv, r):
        d = 0 if r > half else 1
        buf = chain.at[d, kv, r]
        if r in (half - 1, half + 1):
            sums(kv, r, buf)
        else:
            sums(kv, r, term.at[d])
            wait_chain(d, kv, r)
            buf[...] = (buf[...].astype(F32) + term[d]).astype(BF16)
        chain_copy(kv, r).start()

    def compute(r):
        row = lax.rem(z - r + nz, nz)
        prompts(r).wait()
        for u in range(NY):
            w = r * NY + u
            slot = lax.div(jnp.maximum(m_ref[dp, row * NY + lax.rem(y - u + NY, NY)], 0), PACK)
            queries = jnp.concatenate([qb[slot, :, h * HD : (h + 1) * HD] for h in range(heads)], axis=0)
            cotangent = jnp.concatenate([dob[slot, :, h * HD : (h + 1) * HD] for h in range(heads)], axis=0)
            keys = jnp.concatenate([preb[w, 0], ckb[slot]], axis=0)
            values = jnp.concatenate([preb[w, 1], cvb[slot]], axis=0)
            out, dq, dk, dv = attend_slot(len_ref[slot], queries, cotangent, keys, values, heads)
            for h in range(heads):
                ob[w, :, h * HD : (h + 1) * HD] = out[h * tokens : (h + 1) * tokens]
                dqb[w, :, h * HD : (h + 1) * HD] = dq[h * tokens : (h + 1) * tokens]
            g_ref[w, 0] = dk[:prefix]
            g_ref[w, 1] = dv[:prefix]
            tailb[w, 0] = dk[prefix:]
            tailb[w, 1] = dv[prefix:]
        for copy in results(r):
            copy.start()

    def hop(h):
        for kv in range(2):
            for r in (h, nz - h):
                wait_y(kv, r)
            if h == half - 1:
                for u in range(NY):
                    far_copy(kv, u).wait_recv()
            for r in (h, nz - h):
                reduce_block(kv, r)

    def after(i):
        if i == 0:
            for kv in range(2):
                for u in range(NY):
                    far_copy(kv, u).start()
            return
        for kv in range(2):
            send_out(kv, order[i])
        if i >= 4 and i % 2 == 0:
            hop(half + 1 - i // 2)

    def step(i, carry):
        back = lax.div(i + 1, 2)
        sign = 2 * lax.rem(i + 1, 2) - 1
        compute(lax.rem(half + sign * back + nz, nz))
        for j in range(nz):
            pl.when(i == j)(functools.partial(after, j))
        return carry

    for copy in local:
        copy.wait()
    lax.fori_loop(0, nz, step, 0)
    hop(1)
    mine = pl.ds(pl.multiple_of(t * share, share), share)
    own = pl.ds(pl.multiple_of(t * HD, HD), HD)
    for kv in range(2):
        wait_y(kv, 0)
        sums(kv, 0, term.at[0])
        for d in range(2):
            wait_chain(d, kv, 0)
        total[kv] = (term[0] + chain[0, kv, 0].astype(F32) + chain[1, kv, 0].astype(F32)).astype(BF16)
        for j in range(1, n_t):
            piece_copy(kv, j).start()
        (ok_ref, ov_ref)[kv][:, :, own] = total[kv, :, mine, :].astype(F32)
    for kv in range(2):
        for j in range(1, n_t):
            piece_copy(kv, j).wait_recv()
            cols = pl.ds(pl.multiple_of(at_t(-j)[1] * HD, HD), HD)
            (ok_ref, ov_ref)[kv][:, :, cols] = pieces[kv, j].astype(F32)
    for kv in range(2):
        for u in range(NY):
            far_copy(kv, u).wait_send()
        for r in order[1:]:
            for u in range(1, NY):
                out_copy(kv, r, u).wait_send()
            if r:
                chain_copy(kv, r).wait_send()
        for j in range(1, n_t):
            piece_copy(kv, j).wait_send()
    for r in range(nz):
        for copy in results(r):
            copy.wait()


def attend_scatter(n_dp, n_t, table, cont_len, q, do, ck, cv, pre, per, share, cid=1):
    nz = n_dp // NY
    slots, tokens, width = q.shape
    plen = pre.shape[2]
    dma = pltpu.SemaphoreType.DMA
    shape = jax.ShapeDtypeStruct
    anywhere = pl.BlockSpec(memory_space=pl.ANY)
    scalars = pl.BlockSpec(memory_space=pltpu.SMEM)
    part = shape((per, share, n_t * HD), F32)
    wide = (n_dp, tokens, width)
    tails = (n_dp, 2, tokens, HD)
    flops = 12 * n_dp * tokens * (tokens + plen) * width
    return pl.pallas_call(
        functools.partial(attend_scatter_kernel, n_dp, n_t),
        out_shape=(shape(wide, BF16), shape(wide, BF16), shape(tails, BF16), part, part),
        in_specs=[scalars, scalars] + [anywhere] * 5,
        out_specs=[anywhere] * 3 + [pl.BlockSpec(memory_space=pltpu.VMEM)] * 2,
        scratch_shapes=[
            pltpu.VMEM(q.shape, BF16),
            pltpu.VMEM(q.shape, BF16),
            pltpu.VMEM(ck.shape, BF16),
            pltpu.VMEM(ck.shape, BF16),
            pltpu.VMEM(pre.shape, BF16),
            pltpu.VMEM(wide, BF16),
            pltpu.VMEM(wide, BF16),
            pltpu.VMEM(tails, BF16),
            pltpu.VMEM(pre.shape, BF16),
            pltpu.VMEM((nz, NY, 2, plen, HD), BF16),
            pltpu.VMEM((2, NY, plen, HD), BF16),
            pltpu.VMEM((2, 2, nz, per, plen, HD), BF16),
            pltpu.VMEM((2, per, plen, HD), F32),
            pltpu.VMEM((2, per, plen, HD), BF16),
            pltpu.VMEM((2, n_t, per, share, HD), BF16),
            dma((4,)),
            dma((nz,)),
            dma((3, nz)),
            dma((nz, NY, 2)),
            dma((nz, NY, 2)),
            dma((nz, 2)),
            dma((2, NY)),
            dma((2, NY)),
            dma((2, 2, nz)),
            dma((2, 2, nz)),
            dma((2, n_t)),
            dma((2, n_t)),
        ],
        compiler_params=pltpu.CompilerParams(
            collective_id=cid, has_side_effects=True, vmem_limit_bytes=VMEM_LIMIT
        ),
        cost_estimate=pl.CostEstimate(flops=flops, bytes_accessed=4 * q.size * 2, transcendentals=q.size),
        name="attend_scatter",
    )(table, cont_len, q, do, ck, cv, pre)


def finish_kernel(per, named_ref, out_ref, dq_ref, tail_ref, k_ref, v_ref, out, dq, dk, dv, gk, gv, ob, dqb, tb, kb, vb, first, last):
    slots = out.shape[0]
    nz = out_ref.shape[0] // NY
    dp = lax.axis_index("dp")
    z, y = dp // NY, dp % NY
    copy = pltpu.make_async_copy
    moved = ((k_ref, kb, gk), (v_ref, vb, gv))

    def fetch(s, w):
        pairs = ((out_ref, ob), (dq_ref, dqb), (tail_ref, tb))
        return [copy(src.at[w], dst.at[s], first.at[i, s]) for i, (src, dst) in enumerate(pairs)]

    def store(s):
        pairs = ((ob, out), (dqb, dq))
        return [copy(src.at[s], dst.at[s], last.at[i, s]) for i, (src, dst) in enumerate(pairs)]

    def begin(s, carry):
        owner = lax.div(named_ref[dp * slots + s], per)
        row = lax.rem(z - owner // NY + nz, nz)
        for c in fetch(s, row * NY + lax.rem(y - owner % NY + NY, NY)):
            c.start()
        return carry

    def pass_on(s, carry):
        for c in fetch(s, 0):
            c.wait()
        for c in store(s):
            c.start()
        return carry

    def end(s, carry):
        for c in store(s):
            c.wait()
        return carry

    lax.fori_loop(0, slots, begin, 0)
    for i, (src, buf, _) in enumerate(moved):
        copy(src, buf, first.at[3, i]).start()
    lax.fori_loop(0, slots, pass_on, 0)
    ends = [copy(tb.at[:, i], dst, last.at[2, i]) for i, dst in enumerate((dk, dv))]
    for i, (src, buf, dst) in enumerate(moved):
        copy(src, buf, first.at[3, i]).wait()
        ends.append(copy(buf, dst, last.at[3, i]))
    for c in ends:
        c.start()
    lax.fori_loop(0, slots, end, 0)
    for c in ends:
        c.wait()


def finish(per, slots, named, out, dq, tail, gk, gv):
    shape = jax.ShapeDtypeStruct
    anywhere = pl.BlockSpec(memory_space=pl.ANY)
    wide = shape((slots,) + out.shape[1:], BF16)
    thin = shape((slots,) + tail.shape[2:], BF16)
    dma = pltpu.SemaphoreType.DMA
    return pl.pallas_call(
        functools.partial(finish_kernel, per),
        out_shape=(wide, wide, thin, thin, shape(gk.shape, F32), shape(gv.shape, F32)),
        in_specs=[pl.BlockSpec(memory_space=pltpu.SMEM)] + [anywhere] * 5,
        out_specs=[anywhere] * 6,
        scratch_shapes=[
            pltpu.VMEM(wide.shape, BF16),
            pltpu.VMEM(wide.shape, BF16),
            pltpu.VMEM((slots,) + tail.shape[1:], BF16),
            pltpu.VMEM(gk.shape, F32),
            pltpu.VMEM(gv.shape, F32),
            dma((4, slots)),
            dma((4, slots)),
        ],
        compiler_params=pltpu.CompilerParams(vmem_limit_bytes=FINISH_LIMIT),
        name="finish",
    )(named, out, dq, tail, gk, gv)


def dot(a, b, dims):
    return lax.dot_general(a, b, (dims, ((), ())), preferred_element_type=F32)


def attend_slot(length, queries, cotangent, keys, values, heads):
    rows = queries.shape[0]
    count = keys.shape[0]
    tokens = rows // heads
    prefix = count - tokens
    scale = 1.0 / math.sqrt(HD)
    token = lax.rem(lax.broadcasted_iota(jnp.int32, (1, rows), 1), tokens)
    valid = lax.rem(lax.broadcasted_iota(jnp.int32, (rows, 1), 0), tokens) < length
    cotangent = jnp.where(valid, cotangent, jnp.zeros_like(cotangent))
    scores = dot(keys, queries, ((1,), (1,)))
    dweights = dot(values, cotangent, ((1,), (1,)))
    key = lax.broadcasted_iota(jnp.int32, (tokens, rows), 0)
    tail = jnp.where(key <= token, scores[prefix:], NEG)
    scores = jnp.concatenate([scores[:prefix], tail], axis=0)
    top = jnp.max(scores, axis=0, keepdims=True)
    exponent = jnp.exp2((scores - top) * (scale * math.log2(math.e)))
    probs = exponent * (1.0 / jnp.sum(exponent, axis=0, keepdims=True))
    weights = probs.astype(BF16)
    delta = jnp.sum(probs * dweights, axis=0, keepdims=True)
    dscores = (probs * ((dweights - delta) * scale)).astype(BF16)
    out = dot(values, weights, ((0,), (0,))).astype(BF16).T
    out = jnp.where(valid, out, jnp.zeros_like(out))
    dq = dot(keys, dscores, ((0,), (0,))).astype(BF16).T
    dk = dot(dscores, queries, ((1,), (0,))).astype(BF16)
    dv = dot(weights, cotangent, ((1,), (0,))).astype(BF16)
    return out, dq, dk, dv


def on_device(n_dp, n_t, cont_q, cont_k, cont_v, out_grad, prompt_k, prompt_v, cont_len, cont_prompt):
    slots = cont_q.shape[0]
    per, share = prompt_k.shape[:2]
    owner = lax.broadcasted_iota(jnp.int32, (1, 1, n_dp), 2)
    offset = cont_prompt.reshape(n_dp, slots, 1) - owner * per
    slot = lax.broadcasted_iota(jnp.int32, (1, slots, 1), 1)
    table = jnp.max(jnp.where((offset >= 0) & (offset < per), slot * PACK + offset, -1), axis=1)
    pre = gather_prompts(n_dp, n_t, table, prompt_k, prompt_v)
    out, dq, tail, gk, gv = attend_scatter(
        n_dp, n_t, table, cont_len, cont_q, out_grad, cont_k, cont_v, pre, per, share
    )
    return finish(per, slots, cont_prompt, out, dq, tail, gk, gv)


def solution(mesh):
    n_dp, n_t = mesh.shape["dp"], mesh.shape["tensor"]
    return jax.shard_map(
        functools.partial(on_device, n_dp, n_t),
        mesh=mesh,
        in_specs=(
            P("dp", None, "tensor"),
            P("dp", None, "tensor"),
            P("dp", None, "tensor"),
            P("dp", None, "tensor"),
            P("dp", "tensor", None),
            P("dp", "tensor", None),
            P("dp"),
            P(),
        ),
        out_specs=(
            P("dp", None, "tensor"),
            P("dp", None, "tensor"),
            P("dp", None, "tensor"),
            P("dp", None, "tensor"),
            P("dp", "tensor", None),
            P("dp", "tensor", None),
        ),
        check_vma=False,
    )
```

```python
import functools
import math

import jax
import jax.numpy as jnp
from jax import lax
from jax.experimental import pallas as pl
from jax.experimental.pallas import tpu as pltpu
from jax.sharding import PartitionSpec as P

HD = 128
NY = 4
PACK = 8
NEG = -1e30
VMEM_LIMIT = 56 * 2**20
FINISH_LIMIT = 56 * 2**20
MESH = pl.DeviceIdType.MESH
BF16 = jnp.bfloat16
F32 = jnp.float32


def coordinates(n_dp, n_t):
    dp = lax.axis_index("dp")
    t = lax.axis_index("tensor")
    z, y = dp // NY, dp % NY
    nz = n_dp // NY

    def at_z(step):
        return (lax.rem(z + step + nz, nz) * NY + y, t)

    def at_y(step):
        return (z * NY + lax.rem(y + step + NY, NY), t)

    def at_t(step):
        return (dp, lax.rem(t + step + n_t, n_t))

    def at_zy(step, u):
        return (lax.rem(z + step + nz, nz) * NY + lax.rem(y + u + NY, NY), t)

    return z, y, t, at_z, at_y, at_t, at_zy


def greet(devices):
    barrier = pltpu.get_barrier_semaphore()
    for device in devices:
        pl.semaphore_signal(barrier, inc=1, device_id=device, device_id_type=MESH)
    pl.semaphore_wait(barrier, len(devices))


def remote(src, dst, send, recv, device):
    return pltpu.make_async_remote_copy(
        src_ref=src,
        dst_ref=dst,
        send_sem=send,
        recv_sem=recv,
        device_id=device,
        device_id_type=MESH,
    )


def partners(n_t, at_z, at_y, at_t, at_zy):
    return (
        [at_t(j) for j in range(1, n_t)]
        + [at_y(u) for u in range(1, NY)]
        + [at_zy(way, u) for way in (1, -1) for u in range(NY)]
    )


def fused_kernel(
    n_dp, n_t, named_ref, len_ref, q_ref, do_ref, ck_ref, cv_ref, pk_ref, pv_ref, out_ref, dq_ref, tail_ref, ok_ref, ov_ref, *scratch
):
    nz = n_dp // NY
    half = nz // 2
    blocks = [list(scratch[:nz]), list(scratch[nz : 2 * nz])]
    table, picked, qb, dob, ckb, cvb, preb, ob, dqb, tailb, g_ref = scratch[2 * nz : 2 * nz + 11]
    arrived, far, chain, term, total, pieces = scratch[2 * nz + 11 : 2 * nz + 17]
    ins, outs, ys, yr, yl, fs, fr, zs, zr, xs, xr, bs, br, bl, hs, hr, ks, kr = scratch[2 * nz + 17 :]
    z, y, t, at_z, at_y, at_t, at_zy = coordinates(n_dp, n_t)
    per, share = ok_ref.shape[:2]
    slots, tokens, width = q_ref.shape
    heads = width // HD
    prefix = share * n_t
    mine = pl.ds(pl.multiple_of(t * share, share), share)
    own = pl.ds(pl.multiple_of(t * HD, HD), HD)
    local = [
        pltpu.make_async_copy(src, dst, ins.at[i])
        for i, (src, dst) in enumerate(((q_ref, qb), (do_ref, dob), (ck_ref, ckb), (cv_ref, cvb)))
    ]
    owned = [
        pltpu.make_async_copy(ref.at[:, :, own], blocks[kv][0].at[:, mine, :], bl.at[kv])
        for kv, ref in enumerate((pk_ref, pv_ref))
    ]

    def results(r):
        part = pl.ds(r * NY, NY)
        return [
            pltpu.make_async_copy(src.at[part], dst.at[part], outs.at[i, r])
            for i, (src, dst) in enumerate(((ob, out_ref), (dqb, dq_ref), (tailb, tail_ref)))
        ]

    def share_copy(kv, j):
        to = at_t(j)
        cols = pl.ds(pl.multiple_of(to[1] * HD, HD), HD)
        src = (pk_ref, pv_ref)[kv].at[:, :, cols]
        return remote(src, blocks[kv][0].at[:, mine, :], bs.at[kv, j], br.at[kv, j], to)

    def wait_own(kv):
        owned[kv].wait()
        for j in range(1, n_t):
            rows = pl.ds(pl.multiple_of(at_t(-j)[1] * share, share), share)
            src = (pk_ref, pv_ref)[kv].at[:, :, own]
            remote(src, blocks[kv][0].at[:, rows, :], bs.at[kv, j], br.at[kv, j], at_t(j)).wait_recv()

    def block_copy(kv, r, way):
        nxt = (r + way) % nz
        return remote(blocks[kv][r], blocks[kv][nxt], hs.at[kv, nxt], hr.at[kv, nxt], at_z(way))

    def wait_block(kv, r):
        remote(blocks[kv][r], blocks[kv][r], hs.at[kv, r], hr.at[kv, r], at_z(1)).wait_recv()

    def pick_copy(kv, r, u, way=0):
        place = preb.at[r * NY + u, kv]
        return remote(picked.at[r, u, kv], place, ks.at[r, u, kv], kr.at[r, u, kv], at_zy(way, u))

    def spread(kv, r, way=0):
        there = (r + way) % nz
        for u in (2, 1, 3, 0):
            name = table[2, kv * NY + u] if way else table[0, r * NY + u]
            pick = lax.rem(jnp.maximum(name, 0), PACK)
            if u == 0 and way == 0:
                preb[r * NY, kv] = blocks[kv][r][pick]
            else:
                picked[there, u, kv] = blocks[kv][r][pick]
                pick_copy(kv, there, u, way).start()

    def gather(kv, h):
        if h == 0:
            wait_own(kv)
            block_copy(kv, 0, 1).start()
            block_copy(kv, 0, -1).start()
            return
        for r, way in ((h, 1), (nz - h, -1)):
            wait_block(kv, r)
            if h < half - 1:
                block_copy(kv, r, way).start()
            elif kv == (0 if way == 1 else 1):
                spread(kv, r, way)
        for r in (h, nz - h):
            spread(kv, r)

    def entry(device, owner):
        found = jnp.int32(-1)
        for s in range(slots):
            offset = named_ref[device * slots + s] - owner * per
            found = jnp.where((offset >= 0) & (offset < per), s * PACK + offset, found)
        return found

    def fill(r, carry):
        row = lax.rem(z - r + nz, nz) * NY
        for u in range(NY):
            table[0, r * NY + u] = entry(at_y(u)[0], row + y)
            table[1, r * NY + u] = entry(z * NY + y, row + at_y(-u)[0] - z * NY)
        return carry

    def far_copy(kv, u):
        src = g_ref.at[half * NY + u, kv]
        return remote(src, far.at[kv, u], fs.at[kv, u], fr.at[kv, u], at_zy(-1 if kv == 0 else 1, -u))

    def out_copy(kv, r, u):
        return remote(
            g_ref.at[r * NY + u, kv], arrived.at[r, u, kv], ys.at[r, u, kv], yr.at[r, u, kv], at_y(-u)
        )

    def chain_copy(kv, r):
        d = 0 if r > half else 1
        step = 1 if d == 0 else -1
        nxt = (r + step) % nz
        return remote(
            chain.at[d, kv, r], chain.at[d, kv, nxt], zs.at[d, kv, nxt], zr.at[d, kv, nxt], at_z(step)
        )

    def piece_copy(kv, j):
        to = at_t(j)
        rows = pl.ds(pl.multiple_of(to[1] * share, share), share)
        return remote(total.at[kv, :, rows, :], pieces.at[kv, j], xs.at[kv, j], xr.at[kv, j], to)

    def send_out(kv, r):
        for u in (2, 1, 3):
            out_copy(kv, r, u).start()
        pltpu.make_async_copy(g_ref.at[r * NY, kv], arrived.at[r, 0, kv], yl.at[r, kv]).start()

    def wait_y(kv, r):
        pltpu.make_async_copy(g_ref.at[r * NY, kv], arrived.at[r, 0, kv], yl.at[r, kv]).wait()
        for u in range(1, NY):
            out_copy(kv, r, u).wait_recv()

    def sums(kv, r, store):
        parts = [(lax.rem(table[0, r * NY + u], PACK), arrived.at[r, u, kv]) for u in range(NY)]
        if r == (half - 1 if kv == 0 else half + 1):
            parts += [(lax.rem(table[2, kv * NY + u], PACK), far.at[kv, u]) for u in range(NY)]
        for p in range(per):
            acc = None
            for which, ref in parts:
                piece = jnp.where(which == p, ref[...].astype(F32), 0.0)
                acc = piece if acc is None else acc + piece
            store[p] = acc.astype(store.dtype)

    def wait_chain(d, kv, r):
        remote(
            chain.at[d, kv, r], chain.at[d, kv, r], zs.at[d, kv, r], zr.at[d, kv, r], at_z(1)
        ).wait_recv()

    def reduce_block(kv, r):
        d = 0 if r > half else 1
        buf = chain.at[d, kv, r]
        if r in (half - 1, half + 1):
            sums(kv, r, buf)
        else:
            sums(kv, r, term.at[d])
            wait_chain(d, kv, r)
            buf[...] = (buf[...].astype(F32) + term[d]).astype(BF16)
        chain_copy(kv, r).start()

    def compute(r):
        for u in range(1, NY):
            for kv in range(2):
                pick_copy(kv, r, u).wait_recv()
        for u in range(NY):
            w = r * NY + u
            slot = lax.div(jnp.maximum(table[1, w], 0), PACK)
            queries = jnp.concatenate([qb[slot, :, h * HD : (h + 1) * HD] for h in range(heads)], axis=0)
            cotangent = jnp.concatenate([dob[slot, :, h * HD : (h + 1) * HD] for h in range(heads)], axis=0)
            keys = jnp.concatenate([preb[w, 0], ckb[slot]], axis=0)
            values = jnp.concatenate([preb[w, 1], cvb[slot]], axis=0)
            out, dq, dk, dv = attend_slot(len_ref[slot], queries, cotangent, keys, values, heads)
            for h in range(heads):
                ob[w, :, h * HD : (h + 1) * HD] = out[h * tokens : (h + 1) * tokens]
                dqb[w, :, h * HD : (h + 1) * HD] = dq[h * tokens : (h + 1) * tokens]
            g_ref[w, 0] = dk[:prefix]
            g_ref[w, 1] = dv[:prefix]
            tailb[w, 0] = dk[prefix:]
            tailb[w, 1] = dv[prefix:]
        for copy in results(r):
            copy.start()

    def hop(h):
        for kv in range(2):
            for r in (h, nz - h):
                wait_y(kv, r)
            if h == half - 1:
                for u in range(NY):
                    far_copy(kv, u).wait_recv()
            for r in (h, nz - h):
                reduce_block(kv, r)

    for copy in local:
        copy.start()
    for copy in owned:
        copy.start()
    greet(partners(n_t, at_z, at_y, at_t, at_zy))
    for kv in range(2):
        for j in range(1, n_t):
            share_copy(kv, j).start()
    lax.fori_loop(0, nz, fill, 0)
    for kv, way in enumerate((1, -1)):
        row = lax.rem(z - way * (half - 1) + nz, nz)
        for u in range(NY):
            table[2, kv * NY + u] = entry(at_zy(way, u)[0], row * NY + y)
    gather(0, 0)
    gather(1, 0)
    for kv in range(2):
        spread(kv, 0)
    gather(0, 1)
    gather(1, 1)
    for copy in local:
        copy.wait()

    def ahead(i):
        if i in (1, 2, 3, 4):
            gather((i + 1) % 2, (i + 3) // 2)
        elif i == nz - 1:
            for kv in range(2):
                pick_copy(kv, half, 0).wait_recv()

    def after(i):
        if i == 4:
            for kv in range(2):
                send_out(kv, 2)
        elif i in (5, 6):
            for kv in range(2):
                send_out(kv, 3 if i == 5 else 5)
        elif i == nz - 1:
            for kv in range(2):
                for u in range(NY):
                    far_copy(kv, u).start()

    def step(i, carry):
        for j in (1, 2, 3, 4, nz - 1):
            pl.when(i == j)(functools.partial(ahead, j))
        sign = 2 * lax.rem(i, 2) - 1
        compute(lax.rem(sign * lax.div(i + 1, 2) + nz, nz))
        for j in (4, 5, 6, nz - 1):
            pl.when(i == j)(functools.partial(after, j))
        return carry

    lax.fori_loop(0, nz, step, 0)
    for kv in range(2):
        send_out(kv, 6)
    hop(3)
    for kv in range(2):
        for r in (1, 7):
            send_out(kv, r)
    hop(2)
    for kv in range(2):
        send_out(kv, 0)
    hop(1)
    for kv in range(2):
        wait_y(kv, 0)
        sums(kv, 0, term.at[0])
        for d in range(2):
            wait_chain(d, kv, 0)
        total[kv] = (term[0] + chain[0, kv, 0].astype(F32) + chain[1, kv, 0].astype(F32)).astype(BF16)
        for j in range(1, n_t):
            piece_copy(kv, j).start()
        (ok_ref, ov_ref)[kv][:, :, own] = total[kv, :, mine, :].astype(F32)
    for kv in range(2):
        for j in range(1, n_t):
            piece_copy(kv, j).wait_recv()
            cols = pl.ds(pl.multiple_of(at_t(-j)[1] * HD, HD), HD)
            (ok_ref, ov_ref)[kv][:, :, cols] = pieces[kv, j].astype(F32)
    for kv in range(2):
        for j in range(1, n_t):
            share_copy(kv, j).wait_send()
            piece_copy(kv, j).wait_send()
        for u in range(NY):
            far_copy(kv, u).wait_send()
            pick_copy(kv, half, u, 1 if kv == 0 else -1).wait_send()
        for r in range(nz):
            if r == half:
                continue
            for u in range(1, NY):
                pick_copy(kv, r, u).wait_send()
                out_copy(kv, r, u).wait_send()
            if r:
                chain_copy(kv, r).wait_send()
        for r in range(half - 1):
            block_copy(kv, r, 1).wait_send()
            block_copy(kv, (nz - r) % nz, -1).wait_send()
    for r in range(nz):
        for copy in results(r):
            copy.wait()


def fused(n_dp, n_t, named, cont_len, q, do, ck, cv, pk, pv):
    nz = n_dp // NY
    slots, tokens, width = q.shape
    per, share = pk.shape[:2]
    plen = share * n_t
    dma = pltpu.SemaphoreType.DMA
    shape = jax.ShapeDtypeStruct
    anywhere = pl.BlockSpec(memory_space=pl.ANY)
    scalars = pl.BlockSpec(memory_space=pltpu.SMEM)
    part = shape((per, share, n_t * HD), F32)
    wide = (n_dp, tokens, width)
    tails = (n_dp, 2, tokens, HD)
    pairs = (nz, NY, 2, plen, HD)
    flops = 12 * n_dp * tokens * (tokens + plen) * width
    return pl.pallas_call(
        functools.partial(fused_kernel, n_dp, n_t),
        out_shape=(shape(wide, BF16), shape(wide, BF16), shape(tails, BF16), part, part),
        in_specs=[scalars, scalars] + [anywhere] * 6,
        out_specs=[anywhere] * 3 + [pl.BlockSpec(memory_space=pltpu.VMEM)] * 2,
        scratch_shapes=[pltpu.VMEM((per, plen, HD), BF16) for _ in range(2 * nz)]
        + [
            pltpu.SMEM((3, n_dp), jnp.int32),
            pltpu.VMEM(pairs, BF16),
            pltpu.VMEM(q.shape, BF16),
            pltpu.VMEM(q.shape, BF16),
            pltpu.VMEM(ck.shape, BF16),
            pltpu.VMEM(ck.shape, BF16),
            pltpu.VMEM((n_dp, 2, plen, HD), BF16),
            pltpu.VMEM(wide, BF16),
            pltpu.VMEM(wide, BF16),
            pltpu.VMEM(tails, BF16),
            pltpu.VMEM((n_dp, 2, plen, HD), BF16),
            pltpu.VMEM(pairs, BF16),
            pltpu.VMEM((2, NY, plen, HD), BF16),
            pltpu.VMEM((2, 2, nz, per, plen, HD), BF16),
            pltpu.VMEM((2, per, plen, HD), F32),
            pltpu.VMEM((2, per, plen, HD), BF16),
            pltpu.VMEM((2, n_t, per, share, HD), BF16),
            dma((4,)),
            dma((3, nz)),
            dma((nz, NY, 2)),
            dma((nz, NY, 2)),
            dma((nz, 2)),
            dma((2, NY)),
            dma((2, NY)),
            dma((2, 2, nz)),
            dma((2, 2, nz)),
            dma((2, n_t)),
            dma((2, n_t)),
            dma((2, n_t)),
            dma((2, n_t)),
            dma((2,)),
            dma((2, nz)),
            dma((2, nz)),
            dma((nz, NY, 2)),
            dma((nz, NY, 2)),
        ],
        compiler_params=pltpu.CompilerParams(
            collective_id=0, has_side_effects=True, vmem_limit_bytes=VMEM_LIMIT
        ),
        cost_estimate=pl.CostEstimate(flops=flops, bytes_accessed=4 * q.size * 2, transcendentals=q.size),
        name="fused",
    )(named, cont_len, q, do, ck, cv, pk, pv)


def finish_kernel(per, named_ref, out_ref, dq_ref, tail_ref, k_ref, v_ref, out, dq, dk, dv, gk, gv, ob, dqb, tb, kb, vb, first, last):
    slots = out.shape[0]
    nz = out_ref.shape[0] // NY
    dp = lax.axis_index("dp")
    z, y = dp // NY, dp % NY
    copy = pltpu.make_async_copy
    moved = ((k_ref, kb, gk), (v_ref, vb, gv))

    def fetch(s, w):
        pairs = ((out_ref, ob), (dq_ref, dqb), (tail_ref, tb))
        return [copy(src.at[w], dst.at[s], first.at[i, s]) for i, (src, dst) in enumerate(pairs)]

    def store(s):
        pairs = ((ob, out), (dqb, dq))
        return [copy(src.at[s], dst.at[s], last.at[i, s]) for i, (src, dst) in enumerate(pairs)]

    def begin(s, carry):
        owner = lax.div(named_ref[dp * slots + s], per)
        row = lax.rem(z - owner // NY + nz, nz)
        for c in fetch(s, row * NY + lax.rem(y - owner % NY + NY, NY)):
            c.start()
        return carry

    def pass_on(s, carry):
        for c in fetch(s, 0):
            c.wait()
        for c in store(s):
            c.start()
        return carry

    def end(s, carry):
        for c in store(s):
            c.wait()
        return carry

    lax.fori_loop(0, slots, begin, 0)
    for i, (src, buf, _) in enumerate(moved):
        copy(src, buf, first.at[3, i]).start()
    lax.fori_loop(0, slots, pass_on, 0)
    ends = [copy(tb.at[:, i], dst, last.at[2, i]) for i, dst in enumerate((dk, dv))]
    for i, (src, buf, dst) in enumerate(moved):
        copy(src, buf, first.at[3, i]).wait()
        ends.append(copy(buf, dst, last.at[3, i]))
    for c in ends:
        c.start()
    lax.fori_loop(0, slots, end, 0)
    for c in ends:
        c.wait()


def finish(per, slots, named, out, dq, tail, gk, gv):
    shape = jax.ShapeDtypeStruct
    anywhere = pl.BlockSpec(memory_space=pl.ANY)
    wide = shape((slots,) + out.shape[1:], BF16)
    thin = shape((slots,) + tail.shape[2:], BF16)
    dma = pltpu.SemaphoreType.DMA
    return pl.pallas_call(
        functools.partial(finish_kernel, per),
        out_shape=(wide, wide, thin, thin, shape(gk.shape, F32), shape(gv.shape, F32)),
        in_specs=[pl.BlockSpec(memory_space=pltpu.SMEM)] + [anywhere] * 5,
        out_specs=[anywhere] * 6,
        scratch_shapes=[
            pltpu.VMEM(wide.shape, BF16),
            pltpu.VMEM(wide.shape, BF16),
            pltpu.VMEM((slots,) + tail.shape[1:], BF16),
            pltpu.VMEM(gk.shape, F32),
            pltpu.VMEM(gv.shape, F32),
            dma((4, slots)),
            dma((4, slots)),
        ],
        compiler_params=pltpu.CompilerParams(vmem_limit_bytes=FINISH_LIMIT),
        name="finish",
    )(named, out, dq, tail, gk, gv)


def dot(a, b, dims):
    return lax.dot_general(a, b, (dims, ((), ())), preferred_element_type=F32)


def attend_slot(length, queries, cotangent, keys, values, heads):
    rows = queries.shape[0]
    count = keys.shape[0]
    tokens = rows // heads
    prefix = count - tokens
    scale = 1.0 / math.sqrt(HD)
    token = lax.rem(lax.broadcasted_iota(jnp.int32, (1, rows), 1), tokens)
    valid = lax.rem(lax.broadcasted_iota(jnp.int32, (rows, 1), 0), tokens) < length
    cotangent = jnp.where(valid, cotangent, jnp.zeros_like(cotangent))
    scores = dot(keys, queries, ((1,), (1,)))
    dweights = dot(values, cotangent, ((1,), (1,)))
    key = lax.broadcasted_iota(jnp.int32, (tokens, rows), 0)
    tail = jnp.where(key <= token, scores[prefix:], NEG)
    scores = jnp.concatenate([scores[:prefix], tail], axis=0)
    top = jnp.max(scores, axis=0, keepdims=True)
    exponent = jnp.exp2((scores - top) * (scale * math.log2(math.e)))
    probs = exponent * (1.0 / jnp.sum(exponent, axis=0, keepdims=True))
    weights = probs.astype(BF16)
    delta = jnp.sum(probs * dweights, axis=0, keepdims=True)
    dscores = (probs * ((dweights - delta) * scale)).astype(BF16)
    out = dot(values, weights, ((0,), (0,))).astype(BF16).T
    out = jnp.where(valid, out, jnp.zeros_like(out))
    dq = dot(keys, dscores, ((0,), (0,))).astype(BF16).T
    dk = dot(dscores, queries, ((1,), (0,))).astype(BF16)
    dv = dot(weights, cotangent, ((1,), (0,))).astype(BF16)
    return out, dq, dk, dv


def on_device(n_dp, n_t, cont_q, cont_k, cont_v, out_grad, prompt_k, prompt_v, cont_len, cont_prompt):
    out, dq, tail, gk, gv = fused(
        n_dp, n_t, cont_prompt, cont_len, cont_q, out_grad, cont_k, cont_v, prompt_k, prompt_v
    )
    return finish(prompt_k.shape[0], cont_q.shape[0], cont_prompt, out, dq, tail, gk, gv)


def solution(mesh):
    n_dp, n_t = mesh.shape["dp"], mesh.shape["tensor"]
    return jax.shard_map(
        functools.partial(on_device, n_dp, n_t),
        mesh=mesh,
        in_specs=(
            P("dp", None, "tensor"),
            P("dp", None, "tensor"),
            P("dp", None, "tensor"),
            P("dp", None, "tensor"),
            P("dp", "tensor", None),
            P("dp", "tensor", None),
            P("dp"),
            P(),
        ),
        out_specs=(
            P("dp", None, "tensor"),
            P("dp", None, "tensor"),
            P("dp", None, "tensor"),
            P("dp", None, "tensor"),
            P("dp", "tensor", None),
            P("dp", "tensor", None),
        ),
        check_vma=False,
    )
```

```python
import functools
import math

import jax
import jax.numpy as jnp
from jax import lax
from jax.experimental import pallas as pl
from jax.experimental.pallas import tpu as pltpu
from jax.sharding import PartitionSpec as P

HD = 128
NY = 4
PACK = 8
NEG = -1e30
VMEM_LIMIT = 56 * 2**20
FINISH_LIMIT = 56 * 2**20
MESH = pl.DeviceIdType.MESH
BF16 = jnp.bfloat16
F32 = jnp.float32


def coordinates(n_dp, n_t):
    dp = lax.axis_index("dp")
    t = lax.axis_index("tensor")
    z, y = dp // NY, dp % NY
    nz = n_dp // NY

    def at_z(step):
        return (lax.rem(z + step + nz, nz) * NY + y, t)

    def at_y(step):
        return (z * NY + lax.rem(y + step + NY, NY), t)

    def at_t(step):
        return (dp, lax.rem(t + step + n_t, n_t))

    def at_zy(step, u):
        return (lax.rem(z + step + nz, nz) * NY + lax.rem(y + u + NY, NY), t)

    return z, y, t, at_z, at_y, at_t, at_zy


def greet(devices):
    barrier = pltpu.get_barrier_semaphore()
    for device in devices:
        pl.semaphore_signal(barrier, inc=1, device_id=device, device_id_type=MESH)
    pl.semaphore_wait(barrier, len(devices))


def remote(src, dst, send, recv, device):
    return pltpu.make_async_remote_copy(
        src_ref=src,
        dst_ref=dst,
        send_sem=send,
        recv_sem=recv,
        device_id=device,
        device_id_type=MESH,
    )


def partners(n_t, at_z, at_y, at_t, at_zy):
    return (
        [at_t(j) for j in range(1, n_t)]
        + [at_y(u) for u in range(1, NY)]
        + [at_zy(way, u) for way in (1, -1) for u in range(NY)]
    )


def fused_kernel(
    n_dp, n_t, named_ref, len_ref, q_ref, do_ref, ck_ref, cv_ref, pk_ref, pv_ref, out_ref, dq_ref, tail_ref, ok_ref, ov_ref, *scratch
):
    nz = n_dp // NY
    half = nz // 2
    blocks = [list(scratch[:nz]), list(scratch[nz : 2 * nz])]
    table, picked, qb, dob, ckb, cvb, preb, ob, dqb, tailb, g_ref = scratch[2 * nz : 2 * nz + 11]
    arrived, far, chain, term, total, pieces = scratch[2 * nz + 11 : 2 * nz + 17]
    ins, outs, ys, yr, yl, fs, fr, zs, zr, xs, xr, bs, br, bl, hs, hr, ks, kr = scratch[2 * nz + 17 :]
    z, y, t, at_z, at_y, at_t, at_zy = coordinates(n_dp, n_t)
    per, share = ok_ref.shape[:2]
    slots, tokens, width = q_ref.shape
    heads = width // HD
    prefix = share * n_t
    mine = pl.ds(pl.multiple_of(t * share, share), share)
    own = pl.ds(pl.multiple_of(t * HD, HD), HD)
    local = [
        pltpu.make_async_copy(src, dst, ins.at[i])
        for i, (src, dst) in enumerate(((q_ref, qb), (do_ref, dob), (ck_ref, ckb), (cv_ref, cvb)))
    ]
    owned = [
        pltpu.make_async_copy(ref.at[:, :, own], blocks[kv][0].at[:, mine, :], bl.at[kv])
        for kv, ref in enumerate((pk_ref, pv_ref))
    ]

    def results(r):
        part = pl.ds(r * NY, NY)
        return [
            pltpu.make_async_copy(src.at[part], dst.at[part], outs.at[i, r])
            for i, (src, dst) in enumerate(((ob, out_ref), (dqb, dq_ref), (tailb, tail_ref)))
        ]

    def share_copy(kv, j):
        to = at_t(j)
        cols = pl.ds(pl.multiple_of(to[1] * HD, HD), HD)
        src = (pk_ref, pv_ref)[kv].at[:, :, cols]
        return remote(src, blocks[kv][0].at[:, mine, :], bs.at[kv, j], br.at[kv, j], to)

    def wait_own(kv):
        owned[kv].wait()
        for j in range(1, n_t):
            rows = pl.ds(pl.multiple_of(at_t(-j)[1] * share, share), share)
            src = (pk_ref, pv_ref)[kv].at[:, :, own]
            remote(src, blocks[kv][0].at[:, rows, :], bs.at[kv, j], br.at[kv, j], at_t(j)).wait_recv()

    def block_copy(kv, r, way):
        nxt = (r + way) % nz
        return remote(blocks[kv][r], blocks[kv][nxt], hs.at[kv, nxt], hr.at[kv, nxt], at_z(way))

    def wait_block(kv, r):
        remote(blocks[kv][r], blocks[kv][r], hs.at[kv, r], hr.at[kv, r], at_z(1)).wait_recv()

    def pick_copy(kv, r, u, way=0):
        place = preb.at[r * NY + u, kv]
        return remote(picked.at[r, u, kv], place, ks.at[r, u, kv], kr.at[r, u, kv], at_zy(way, u))

    def spread(kv, r, way=0):
        there = (r + way) % nz
        for u in (2, 1, 3, 0):
            name = table[2, kv * NY + u] if way else table[0, r * NY + u]
            pick = lax.rem(jnp.maximum(name, 0), PACK)
            if u == 0 and way == 0:
                preb[r * NY, kv] = blocks[kv][r][pick]
            else:
                picked[there, u, kv] = blocks[kv][r][pick]
                pick_copy(kv, there, u, way).start()

    def gather(kv, h):
        if h == 0:
            wait_own(kv)
            block_copy(kv, 0, 1).start()
            block_copy(kv, 0, -1).start()
            return
        for r, way in ((h, 1), (nz - h, -1)):
            wait_block(kv, r)
            if h < half - 1:
                block_copy(kv, r, way).start()
            elif kv == (0 if way == 1 else 1):
                spread(kv, r, way)
        for r in (h, nz - h):
            spread(kv, r)

    def entry(device, owner):
        found = jnp.int32(-1)
        for s in range(slots):
            offset = named_ref[device * slots + s] - owner * per
            found = jnp.where((offset >= 0) & (offset < per), s * PACK + offset, found)
        return found

    def fill(r, carry):
        row = lax.rem(z - r + nz, nz) * NY
        for u in range(NY):
            table[0, r * NY + u] = entry(at_y(u)[0], row + y)
            table[1, r * NY + u] = entry(z * NY + y, row + at_y(-u)[0] - z * NY)
        return carry

    def far_copy(kv, u):
        src = g_ref.at[half * NY + u, kv]
        return remote(src, far.at[kv, u], fs.at[kv, u], fr.at[kv, u], at_zy(-1 if kv == 0 else 1, -u))

    def out_copy(kv, r, u):
        return remote(
            g_ref.at[r * NY + u, kv], arrived.at[r, u, kv], ys.at[r, u, kv], yr.at[r, u, kv], at_y(-u)
        )

    def chain_copy(kv, r):
        d = 0 if r > half else 1
        step = 1 if d == 0 else -1
        nxt = (r + step) % nz
        return remote(
            chain.at[d, kv, r], chain.at[d, kv, nxt], zs.at[d, kv, nxt], zr.at[d, kv, nxt], at_z(step)
        )

    def piece_copy(kv, j):
        to = at_t(j)
        rows = pl.ds(pl.multiple_of(to[1] * share, share), share)
        return remote(total.at[kv, :, rows, :], pieces.at[kv, j], xs.at[kv, j], xr.at[kv, j], to)

    def send_out(kv, r):
        for u in (2, 1, 3):
            out_copy(kv, r, u).start()
        pltpu.make_async_copy(g_ref.at[r * NY, kv], arrived.at[r, 0, kv], yl.at[r, kv]).start()

    def wait_y(kv, r):
        pltpu.make_async_copy(g_ref.at[r * NY, kv], arrived.at[r, 0, kv], yl.at[r, kv]).wait()
        for u in range(1, NY):
            out_copy(kv, r, u).wait_recv()

    def sums(kv, r, store):
        parts = [(lax.rem(table[0, r * NY + u], PACK), arrived.at[r, u, kv]) for u in range(NY)]
        if r == (half - 1 if kv == 0 else half + 1):
            parts += [(lax.rem(table[2, kv * NY + u], PACK), far.at[kv, u]) for u in range(NY)]
        for p in range(per):
            acc = None
            for which, ref in parts:
                piece = jnp.where(which == p, ref[...].astype(F32), 0.0)
                acc = piece if acc is None else acc + piece
            store[p] = acc.astype(store.dtype)

    def wait_chain(d, kv, r):
        remote(
            chain.at[d, kv, r], chain.at[d, kv, r], zs.at[d, kv, r], zr.at[d, kv, r], at_z(1)
        ).wait_recv()

    def reduce_block(kv, r):
        d = 0 if r > half else 1
        buf = chain.at[d, kv, r]
        if r in (half - 1, half + 1):
            sums(kv, r, buf)
        else:
            sums(kv, r, term.at[d])
            wait_chain(d, kv, r)
            buf[...] = (buf[...].astype(F32) + term[d]).astype(BF16)
        chain_copy(kv, r).start()

    def compute(r):
        for u in range(1, NY):
            for kv in range(2):
                pick_copy(kv, r, u).wait_recv()
        for u in range(NY):
            w = r * NY + u
            slot = lax.div(jnp.maximum(table[1, w], 0), PACK)
            queries = jnp.concatenate([qb[slot, :, h * HD : (h + 1) * HD] for h in range(heads)], axis=0)
            cotangent = jnp.concatenate([dob[slot, :, h * HD : (h + 1) * HD] for h in range(heads)], axis=0)
            keys = jnp.concatenate([preb[w, 0], ckb[slot]], axis=0)
            values = jnp.concatenate([preb[w, 1], cvb[slot]], axis=0)
            out, dq, dk, dv = attend_slot(len_ref[slot], queries, cotangent, keys, values, heads)
            for h in range(heads):
                ob[w, :, h * HD : (h + 1) * HD] = out[h * tokens : (h + 1) * tokens]
                dqb[w, :, h * HD : (h + 1) * HD] = dq[h * tokens : (h + 1) * tokens]
            g_ref[w, 0] = dk[:prefix]
            g_ref[w, 1] = dv[:prefix]
            tailb[w, 0] = dk[prefix:]
            tailb[w, 1] = dv[prefix:]
        for copy in results(r):
            copy.start()

    def hop(h):
        for kv, r in ((1, h), (0, nz - h), (0, h), (1, nz - h)):
            wait_y(kv, r)
            if h == half - 1 and kv == (0 if r == h else 1):
                for u in range(NY):
                    far_copy(kv, u).wait_recv()
            reduce_block(kv, r)

    for copy in owned:
        copy.start()
    greet(partners(n_t, at_z, at_y, at_t, at_zy))
    for kv in range(2):
        for j in range(1, n_t):
            share_copy(kv, j).start()
    lax.fori_loop(0, nz, fill, 0)
    for kv, way in enumerate((1, -1)):
        row = lax.rem(z - way * (half - 1) + nz, nz)
        for u in range(NY):
            table[2, kv * NY + u] = entry(at_zy(way, u)[0], row * NY + y)
    gather(0, 0)
    gather(1, 0)
    for kv in range(2):
        spread(kv, 0)
    for copy in local:
        copy.start()
    gather(0, 1)
    gather(1, 1)
    for copy in local:
        copy.wait()

    def ahead(i):
        if i in (1, 2):
            gather(i - 1, 2)
        elif i == 3:
            gather(0, 3)
            gather(1, 3)
        elif i == nz - 1:
            for kv in range(2):
                pick_copy(kv, half, 0).wait_recv()

    def after(i):
        if i == 5:
            send_out(1, 3)
            send_out(0, 3)
        elif i == 6:
            for r in (5, 2):
                for kv in range(2):
                    send_out(kv, r)
        elif i == nz - 1:
            for kv in range(2):
                for u in range(NY):
                    far_copy(kv, u).start()

    def step(i, carry):
        for j in (1, 2, 3, nz - 1):
            pl.when(i == j)(functools.partial(ahead, j))
        sign = 2 * lax.rem(i, 2) - 1
        compute(lax.rem(sign * lax.div(i + 1, 2) + nz, nz))
        for j in (5, 6, nz - 1):
            pl.when(i == j)(functools.partial(after, j))
        return carry

    lax.fori_loop(0, nz, step, 0)
    for kv in range(2):
        send_out(kv, 6)
    hop(3)
    for kv in range(2):
        for r in (1, 7):
            send_out(kv, r)
    hop(2)
    for kv in range(2):
        send_out(kv, 0)
    for kv in range(2):
        for j in range(1, n_t):
            share_copy(kv, j).wait_send()
        for u in range(NY):
            far_copy(kv, u).wait_send()
            pick_copy(kv, half, u, 1 if kv == 0 else -1).wait_send()
        for r in range(nz):
            if r == half:
                continue
            for u in range(1, NY):
                pick_copy(kv, r, u).wait_send()
                if r:
                    out_copy(kv, r, u).wait_send()
        for r in range(half - 1):
            block_copy(kv, r, 1).wait_send()
            block_copy(kv, (nz - r) % nz, -1).wait_send()
    for r in range(nz):
        for copy in results(r):
            copy.wait()
    hop(1)
    for kv in range(2):
        for u in range(1, NY):
            out_copy(kv, 0, u).wait_send()
    for kv in range(2):
        wait_y(kv, 0)
        sums(kv, 0, term.at[0])
        for d in range(2):
            wait_chain(d, kv, 0)
        total[kv] = (term[0] + chain[0, kv, 0].astype(F32) + chain[1, kv, 0].astype(F32)).astype(BF16)
        for j in range(1, n_t):
            piece_copy(kv, j).start()
        (ok_ref, ov_ref)[kv][:, :, own] = total[kv, :, mine, :].astype(F32)
    for kv in range(2):
        for j in range(1, n_t):
            piece_copy(kv, j).wait_recv()
            cols = pl.ds(pl.multiple_of(at_t(-j)[1] * HD, HD), HD)
            (ok_ref, ov_ref)[kv][:, :, cols] = pieces[kv, j].astype(F32)
    for kv in range(2):
        for j in range(1, n_t):
            piece_copy(kv, j).wait_send()
        for r in (h for h in range(1, nz) if h != half):
            chain_copy(kv, r).wait_send()


def fused(n_dp, n_t, named, cont_len, q, do, ck, cv, pk, pv):
    nz = n_dp // NY
    slots, tokens, width = q.shape
    per, share = pk.shape[:2]
    plen = share * n_t
    dma = pltpu.SemaphoreType.DMA
    shape = jax.ShapeDtypeStruct
    anywhere = pl.BlockSpec(memory_space=pl.ANY)
    scalars = pl.BlockSpec(memory_space=pltpu.SMEM)
    part = shape((per, share, n_t * HD), F32)
    wide = (n_dp, tokens, width)
    tails = (n_dp, 2, tokens, HD)
    pairs = (nz, NY, 2, plen, HD)
    flops = 12 * n_dp * tokens * (tokens + plen) * width
    return pl.pallas_call(
        functools.partial(fused_kernel, n_dp, n_t),
        out_shape=(shape(wide, BF16), shape(wide, BF16), shape(tails, BF16), part, part),
        in_specs=[scalars, scalars] + [anywhere] * 6,
        out_specs=[anywhere] * 3 + [pl.BlockSpec(memory_space=pltpu.VMEM)] * 2,
        scratch_shapes=[pltpu.VMEM((per, plen, HD), BF16) for _ in range(2 * nz)]
        + [
            pltpu.SMEM((3, n_dp), jnp.int32),
            pltpu.VMEM(pairs, BF16),
            pltpu.VMEM(q.shape, BF16),
            pltpu.VMEM(q.shape, BF16),
            pltpu.VMEM(ck.shape, BF16),
            pltpu.VMEM(ck.shape, BF16),
            pltpu.VMEM((n_dp, 2, plen, HD), BF16),
            pltpu.VMEM(wide, BF16),
            pltpu.VMEM(wide, BF16),
            pltpu.VMEM(tails, BF16),
            pltpu.VMEM((n_dp, 2, plen, HD), BF16),
            pltpu.VMEM(pairs, BF16),
            pltpu.VMEM((2, NY, plen, HD), BF16),
            pltpu.VMEM((2, 2, nz, per, plen, HD), BF16),
            pltpu.VMEM((2, per, plen, HD), F32),
            pltpu.VMEM((2, per, plen, HD), BF16),
            pltpu.VMEM((2, n_t, per, share, HD), BF16),
            dma((4,)),
            dma((3, nz)),
            dma((nz, NY, 2)),
            dma((nz, NY, 2)),
            dma((nz, 2)),
            dma((2, NY)),
            dma((2, NY)),
            dma((2, 2, nz)),
            dma((2, 2, nz)),
            dma((2, n_t)),
            dma((2, n_t)),
            dma((2, n_t)),
            dma((2, n_t)),
            dma((2,)),
            dma((2, nz)),
            dma((2, nz)),
            dma((nz, NY, 2)),
            dma((nz, NY, 2)),
        ],
        compiler_params=pltpu.CompilerParams(
            collective_id=0, has_side_effects=True, vmem_limit_bytes=VMEM_LIMIT
        ),
        cost_estimate=pl.CostEstimate(flops=flops, bytes_accessed=4 * q.size * 2, transcendentals=q.size),
        name="fused",
    )(named, cont_len, q, do, ck, cv, pk, pv)


def finish_kernel(per, named_ref, out_ref, dq_ref, tail_ref, k_ref, v_ref, out, dq, dk, dv, gk, gv, ob, dqb, tb, kb, vb, first, last):
    slots = out.shape[0]
    nz = out_ref.shape[0] // NY
    dp = lax.axis_index("dp")
    z, y = dp // NY, dp % NY
    copy = pltpu.make_async_copy
    moved = ((k_ref, kb, gk), (v_ref, vb, gv))

    def fetch(s, w):
        pairs = ((out_ref, ob), (dq_ref, dqb), (tail_ref, tb))
        return [copy(src.at[w], dst.at[s], first.at[i, s]) for i, (src, dst) in enumerate(pairs)]

    def store(s):
        pairs = ((ob, out), (dqb, dq))
        return [copy(src.at[s], dst.at[s], last.at[i, s]) for i, (src, dst) in enumerate(pairs)]

    def begin(s, carry):
        owner = lax.div(named_ref[dp * slots + s], per)
        row = lax.rem(z - owner // NY + nz, nz)
        for c in fetch(s, row * NY + lax.rem(y - owner % NY + NY, NY)):
            c.start()
        return carry

    def pass_on(s, carry):
        for c in fetch(s, 0):
            c.wait()
        for c in store(s):
            c.start()
        return carry

    def end(s, carry):
        for c in store(s):
            c.wait()
        return carry

    lax.fori_loop(0, slots, begin, 0)
    for i, (src, buf, _) in enumerate(moved):
        copy(src, buf, first.at[3, i]).start()
    lax.fori_loop(0, slots, pass_on, 0)
    ends = [copy(tb.at[:, i], dst, last.at[2, i]) for i, dst in enumerate((dk, dv))]
    for i, (src, buf, dst) in enumerate(moved):
        copy(src, buf, first.at[3, i]).wait()
        ends.append(copy(buf, dst, last.at[3, i]))
    for c in ends:
        c.start()
    lax.fori_loop(0, slots, end, 0)
    for c in ends:
        c.wait()


def finish(per, slots, named, out, dq, tail, gk, gv):
    shape = jax.ShapeDtypeStruct
    anywhere = pl.BlockSpec(memory_space=pl.ANY)
    wide = shape((slots,) + out.shape[1:], BF16)
    thin = shape((slots,) + tail.shape[2:], BF16)
    dma = pltpu.SemaphoreType.DMA
    return pl.pallas_call(
        functools.partial(finish_kernel, per),
        out_shape=(wide, wide, thin, thin, shape(gk.shape, F32), shape(gv.shape, F32)),
        in_specs=[pl.BlockSpec(memory_space=pltpu.SMEM)] + [anywhere] * 5,
        out_specs=[anywhere] * 6,
        scratch_shapes=[
            pltpu.VMEM(wide.shape, BF16),
            pltpu.VMEM(wide.shape, BF16),
            pltpu.VMEM((slots,) + tail.shape[1:], BF16),
            pltpu.VMEM(gk.shape, F32),
            pltpu.VMEM(gv.shape, F32),
            dma((4, slots)),
            dma((4, slots)),
        ],
        compiler_params=pltpu.CompilerParams(vmem_limit_bytes=FINISH_LIMIT),
        name="finish",
    )(named, out, dq, tail, gk, gv)


def dot(a, b, dims):
    return lax.dot_general(a, b, (dims, ((), ())), preferred_element_type=F32)


def attend_slot(length, queries, cotangent, keys, values, heads):
    rows = queries.shape[0]
    count = keys.shape[0]
    tokens = rows // heads
    prefix = count - tokens
    scale = 1.0 / math.sqrt(HD)
    token = lax.rem(lax.broadcasted_iota(jnp.int32, (1, rows), 1), tokens)
    valid = lax.rem(lax.broadcasted_iota(jnp.int32, (rows, 1), 0), tokens) < length
    cotangent = jnp.where(valid, cotangent, jnp.zeros_like(cotangent))
    scores = dot(keys, queries, ((1,), (1,)))
    dweights = dot(values, cotangent, ((1,), (1,)))
    key = lax.broadcasted_iota(jnp.int32, (tokens, rows), 0)
    tail = jnp.where(key <= token, scores[prefix:], NEG)
    scores = jnp.concatenate([scores[:prefix], tail], axis=0)
    top = jnp.max(scores, axis=0, keepdims=True)
    exponent = jnp.exp2((scores - top) * (scale * math.log2(math.e)))
    probs = exponent * (1.0 / jnp.sum(exponent, axis=0, keepdims=True))
    weights = probs.astype(BF16)
    delta = jnp.sum(probs * dweights, axis=0, keepdims=True)
    dscores = (probs * ((dweights - delta) * scale)).astype(BF16)
    out = dot(values, weights, ((0,), (0,))).astype(BF16).T
    out = jnp.where(valid, out, jnp.zeros_like(out))
    dq = dot(keys, dscores, ((0,), (0,))).astype(BF16).T
    dk = dot(dscores, queries, ((1,), (0,))).astype(BF16)
    dv = dot(weights, cotangent, ((1,), (0,))).astype(BF16)
    return out, dq, dk, dv


def on_device(n_dp, n_t, cont_q, cont_k, cont_v, out_grad, prompt_k, prompt_v, cont_len, cont_prompt):
    out, dq, tail, gk, gv = fused(
        n_dp, n_t, cont_prompt, cont_len, cont_q, out_grad, cont_k, cont_v, prompt_k, prompt_v
    )
    return finish(prompt_k.shape[0], cont_q.shape[0], cont_prompt, out, dq, tail, gk, gv)


def solution(mesh):
    n_dp, n_t = mesh.shape["dp"], mesh.shape["tensor"]
    return jax.shard_map(
        functools.partial(on_device, n_dp, n_t),
        mesh=mesh,
        in_specs=(
            P("dp", None, "tensor"),
            P("dp", None, "tensor"),
            P("dp", None, "tensor"),
            P("dp", None, "tensor"),
            P("dp", "tensor", None),
            P("dp", "tensor", None),
            P("dp"),
            P(),
        ),
        out_specs=(
            P("dp", None, "tensor"),
            P("dp", None, "tensor"),
            P("dp", None, "tensor"),
            P("dp", None, "tensor"),
            P("dp", "tensor", None),
            P("dp", "tensor", None),
        ),
        check_vma=False,
    )
```

```python
import functools
import math

import jax
import jax.numpy as jnp
from jax import lax
from jax.experimental import pallas as pl
from jax.experimental.pallas import tpu as pltpu
from jax.sharding import PartitionSpec as P

HD = 128
NY = 4
PACK = 8
NEG = -1e30
VMEM_LIMIT = 56 * 2**20
FINISH_LIMIT = 56 * 2**20
MESH = pl.DeviceIdType.MESH
BF16 = jnp.bfloat16
F32 = jnp.float32


def coordinates(n_dp, n_t):
    dp = lax.axis_index("dp")
    t = lax.axis_index("tensor")
    z, y = dp // NY, dp % NY
    nz = n_dp // NY

    def at_z(step):
        return (lax.rem(z + step + nz, nz) * NY + y, t)

    def at_y(step):
        return (z * NY + lax.rem(y + step + NY, NY), t)

    def at_t(step):
        return (dp, lax.rem(t + step + n_t, n_t))

    def at_zy(step, u):
        return (lax.rem(z + step + nz, nz) * NY + lax.rem(y + u + NY, NY), t)

    return z, y, t, at_z, at_y, at_t, at_zy


def greet(devices):
    barrier = pltpu.get_barrier_semaphore()
    for device in devices:
        pl.semaphore_signal(barrier, inc=1, device_id=device, device_id_type=MESH)
    pl.semaphore_wait(barrier, len(devices))


def remote(src, dst, send, recv, device):
    return pltpu.make_async_remote_copy(
        src_ref=src,
        dst_ref=dst,
        send_sem=send,
        recv_sem=recv,
        device_id=device,
        device_id_type=MESH,
    )


def partners(n_t, at_z, at_y, at_t, at_zy):
    return (
        [at_t(j) for j in range(1, n_t)]
        + [at_y(u) for u in range(1, NY)]
        + [at_zy(way, u) for way in (1, -1) for u in range(NY)]
    )


def fused_kernel(
    n_dp, n_t, named_ref, len_ref, q_ref, do_ref, ck_ref, cv_ref, pk_ref, pv_ref, out_ref, dq_ref, tail_ref, ok_ref, ov_ref, *scratch
):
    nz = n_dp // NY
    half = nz // 2
    blocks = [list(scratch[:nz]), list(scratch[nz : 2 * nz])]
    table, picked, qb, dob, ckb, cvb, preb, ob, dqb, tailb, g_ref = scratch[2 * nz : 2 * nz + 11]
    arrived, far, chain, term, total, pieces = scratch[2 * nz + 11 : 2 * nz + 17]
    ins, outs, ys, yr, yl, fs, fr, zs, zr, xs, xr, bs, br, bl, hs, hr, ks, kr = scratch[2 * nz + 17 :]
    z, y, t, at_z, at_y, at_t, at_zy = coordinates(n_dp, n_t)
    per, share = ok_ref.shape[:2]
    slots, tokens, width = q_ref.shape
    heads = width // HD
    prefix = share * n_t
    mine = pl.ds(pl.multiple_of(t * share, share), share)
    own = pl.ds(pl.multiple_of(t * HD, HD), HD)
    local = [
        pltpu.make_async_copy(src, dst, ins.at[i])
        for i, (src, dst) in enumerate(((q_ref, qb), (do_ref, dob), (ck_ref, ckb), (cv_ref, cvb)))
    ]
    owned = [
        pltpu.make_async_copy(ref.at[:, :, own], blocks[kv][0].at[:, mine, :], bl.at[kv])
        for kv, ref in enumerate((pk_ref, pv_ref))
    ]

    def results(r):
        part = pl.ds(r * NY, NY)
        return [
            pltpu.make_async_copy(src.at[part], dst.at[part], outs.at[i, r])
            for i, (src, dst) in enumerate(((ob, out_ref), (dqb, dq_ref), (tailb, tail_ref)))
        ]

    def share_copy(kv, j):
        to = at_t(j)
        cols = pl.ds(pl.multiple_of(to[1] * HD, HD), HD)
        src = (pk_ref, pv_ref)[kv].at[:, :, cols]
        return remote(src, blocks[kv][0].at[:, mine, :], bs.at[kv, j], br.at[kv, j], to)

    def wait_own(kv):
        owned[kv].wait()
        for j in range(1, n_t):
            rows = pl.ds(pl.multiple_of(at_t(-j)[1] * share, share), share)
            src = (pk_ref, pv_ref)[kv].at[:, :, own]
            remote(src, blocks[kv][0].at[:, rows, :], bs.at[kv, j], br.at[kv, j], at_t(j)).wait_recv()

    def block_copy(kv, r, way):
        nxt = (r + way) % nz
        return remote(blocks[kv][r], blocks[kv][nxt], hs.at[kv, nxt], hr.at[kv, nxt], at_z(way))

    def wait_block(kv, r):
        remote(blocks[kv][r], blocks[kv][r], hs.at[kv, r], hr.at[kv, r], at_z(1)).wait_recv()

    def pick_copy(kv, r, u, way=0):
        place = preb.at[r * NY + u, kv]
        return remote(picked.at[r, u, kv], place, ks.at[r, u, kv], kr.at[r, u, kv], at_zy(way, u))

    def spread(kv, r, way=0):
        there = (r + way) % nz
        for u in (2, 1, 3, 0):
            name = table[2, kv * NY + u] if way else table[0, r * NY + u]
            pick = lax.rem(jnp.maximum(name, 0), PACK)
            if u == 0 and way == 0:
                preb[r * NY, kv] = blocks[kv][r][pick]
            else:
                picked[there, u, kv] = blocks[kv][r][pick]
                pick_copy(kv, there, u, way).start()

    def gather(kv, h):
        if h == 0:
            wait_own(kv)
            block_copy(kv, 0, 1).start()
            block_copy(kv, 0, -1).start()
            return
        for r, way in ((h, 1), (nz - h, -1)):
            wait_block(kv, r)
            if h < half - 1:
                block_copy(kv, r, way).start()
        for r in (h, nz - h):
            spread(kv, r)
        if h == half - 1:
            spread(kv, h if kv == 0 else nz - h, 1 if kv == 0 else -1)

    def entry(device, owner):
        found = jnp.int32(-1)
        for s in range(slots):
            offset = named_ref[device * slots + s] - owner * per
            found = jnp.where((offset >= 0) & (offset < per), s * PACK + offset, found)
        return found

    def fill(r, carry):
        row = lax.rem(z - r + nz, nz) * NY
        for u in range(NY):
            table[0, r * NY + u] = entry(at_y(u)[0], row + y)
            table[1, r * NY + u] = entry(z * NY + y, row + at_y(-u)[0] - z * NY)
        return carry

    def far_copy(kv, u):
        src = g_ref.at[half * NY + u, kv]
        return remote(src, far.at[kv, u], fs.at[kv, u], fr.at[kv, u], at_zy(-1 if kv == 0 else 1, -u))

    def out_copy(kv, r, u):
        return remote(
            g_ref.at[r * NY + u, kv], arrived.at[r, u, kv], ys.at[r, u, kv], yr.at[r, u, kv], at_y(-u)
        )

    def chain_copy(kv, r):
        d = 0 if r > half else 1
        step = 1 if d == 0 else -1
        nxt = (r + step) % nz
        return remote(
            chain.at[d, kv, r], chain.at[d, kv, nxt], zs.at[d, kv, nxt], zr.at[d, kv, nxt], at_z(step)
        )

    def piece_copy(kv, j):
        to = at_t(j)
        rows = pl.ds(pl.multiple_of(to[1] * share, share), share)
        return remote(total.at[kv, :, rows, :], pieces.at[kv, j], xs.at[kv, j], xr.at[kv, j], to)

    def send_out(kv, r):
        for u in (2, 1, 3):
            out_copy(kv, r, u).start()
        pltpu.make_async_copy(g_ref.at[r * NY, kv], arrived.at[r, 0, kv], yl.at[r, kv]).start()

    def wait_y(kv, r):
        pltpu.make_async_copy(g_ref.at[r * NY, kv], arrived.at[r, 0, kv], yl.at[r, kv]).wait()
        for u in range(1, NY):
            out_copy(kv, r, u).wait_recv()

    def sums(kv, r, store):
        parts = [(lax.rem(table[0, r * NY + u], PACK), arrived.at[r, u, kv]) for u in range(NY)]
        if r == (half - 1 if kv == 0 else half + 1):
            parts += [(lax.rem(table[2, kv * NY + u], PACK), far.at[kv, u]) for u in range(NY)]
        for p in range(per):
            acc = None
            for which, ref in parts:
                piece = jnp.where(which == p, ref[...].astype(F32), 0.0)
                acc = piece if acc is None else acc + piece
            store[p] = acc.astype(store.dtype)

    def wait_chain(d, kv, r):
        remote(
            chain.at[d, kv, r], chain.at[d, kv, r], zs.at[d, kv, r], zr.at[d, kv, r], at_z(1)
        ).wait_recv()

    def reduce_block(kv, r):
        d = 0 if r > half else 1
        buf = chain.at[d, kv, r]
        if r in (half - 1, half + 1):
            sums(kv, r, buf)
        else:
            sums(kv, r, term.at[d])
            wait_chain(d, kv, r)
            buf[...] = (buf[...].astype(F32) + term[d]).astype(BF16)
        chain_copy(kv, r).start()

    def compute(r):
        for u in range(1, NY):
            for kv in range(2):
                pick_copy(kv, r, u).wait_recv()
        for u in range(NY):
            w = r * NY + u
            slot = lax.div(jnp.maximum(table[1, w], 0), PACK)
            queries = jnp.concatenate([qb[slot, :, h * HD : (h + 1) * HD] for h in range(heads)], axis=0)
            cotangent = jnp.concatenate([dob[slot, :, h * HD : (h + 1) * HD] for h in range(heads)], axis=0)
            keys = jnp.concatenate([preb[w, 0], ckb[slot]], axis=0)
            values = jnp.concatenate([preb[w, 1], cvb[slot]], axis=0)
            out, dq, dk, dv = attend_slot(len_ref[slot], queries, cotangent, keys, values, heads)
            for h in range(heads):
                ob[w, :, h * HD : (h + 1) * HD] = out[h * tokens : (h + 1) * tokens]
                dqb[w, :, h * HD : (h + 1) * HD] = dq[h * tokens : (h + 1) * tokens]
            g_ref[w, 0] = dk[:prefix]
            g_ref[w, 1] = dv[:prefix]
            tailb[w, 0] = dk[prefix:]
            tailb[w, 1] = dv[prefix:]
        for copy in results(r):
            copy.start()

    def hop(h):
        for kv, r in ((1, h), (0, nz - h), (0, h), (1, nz - h)):
            wait_y(kv, r)
            if h == half - 1 and kv == (0 if r == h else 1):
                for u in range(NY):
                    far_copy(kv, u).wait_recv()
            reduce_block(kv, r)

    for copy in owned:
        copy.start()
    greet(partners(n_t, at_z, at_y, at_t, at_zy))
    for kv in range(2):
        for j in range(1, n_t):
            share_copy(kv, j).start()
    lax.fori_loop(0, nz, fill, 0)
    for kv, way in enumerate((1, -1)):
        row = lax.rem(z - way * (half - 1) + nz, nz)
        for u in range(NY):
            table[2, kv * NY + u] = entry(at_zy(way, u)[0], row * NY + y)
    gather(0, 0)
    gather(1, 0)
    for kv in range(2):
        spread(kv, 0)
    for copy in local:
        copy.start()
    gather(0, 1)
    gather(1, 1)
    for copy in local:
        copy.wait()

    def ahead(i):
        if i in (1, 2):
            gather(i - 1, 2)
        elif i == 3:
            gather(0, 3)
            gather(1, 3)
        elif i == nz - 1:
            for kv in range(2):
                pick_copy(kv, half, 0).wait_recv()

    def after(i):
        if i == 5:
            send_out(1, 3)
            send_out(0, 3)
        elif i == 6:
            for r in (5, 2):
                for kv in range(2):
                    send_out(kv, r)
        elif i == nz - 1:
            for kv in range(2):
                for u in range(NY):
                    far_copy(kv, u).start()

    def step(i, carry):
        for j in (1, 2, 3, nz - 1):
            pl.when(i == j)(functools.partial(ahead, j))
        sign = 2 * lax.rem(i, 2) - 1
        compute(lax.rem(sign * lax.div(i + 1, 2) + nz, nz))
        for j in (5, 6, nz - 1):
            pl.when(i == j)(functools.partial(after, j))
        return carry

    lax.fori_loop(0, nz, step, 0)
    for kv in range(2):
        send_out(kv, 6)
    hop(3)
    for kv in range(2):
        for r in (1, 7):
            send_out(kv, r)
    hop(2)
    for kv in range(2):
        send_out(kv, 0)
    for kv in range(2):
        for j in range(1, n_t):
            share_copy(kv, j).wait_send()
        for u in range(NY):
            far_copy(kv, u).wait_send()
            pick_copy(kv, half, u, 1 if kv == 0 else -1).wait_send()
        for r in range(nz):
            if r == half:
                continue
            for u in range(1, NY):
                pick_copy(kv, r, u).wait_send()
                if r:
                    out_copy(kv, r, u).wait_send()
        for r in range(half - 1):
            block_copy(kv, r, 1).wait_send()
            block_copy(kv, (nz - r) % nz, -1).wait_send()
    for r in range(nz):
        for copy in results(r):
            copy.wait()
    hop(1)
    for kv in range(2):
        for u in range(1, NY):
            out_copy(kv, 0, u).wait_send()
    for kv in range(2):
        wait_y(kv, 0)
        sums(kv, 0, term.at[0])
        for d in range(2):
            wait_chain(d, kv, 0)
        total[kv] = (term[0] + chain[0, kv, 0].astype(F32) + chain[1, kv, 0].astype(F32)).astype(BF16)
        for j in range(1, n_t):
            piece_copy(kv, j).start()
        (ok_ref, ov_ref)[kv][:, :, own] = total[kv, :, mine, :].astype(F32)
    for kv in range(2):
        for j in range(1, n_t):
            piece_copy(kv, j).wait_recv()
            cols = pl.ds(pl.multiple_of(at_t(-j)[1] * HD, HD), HD)
            (ok_ref, ov_ref)[kv][:, :, cols] = pieces[kv, j].astype(F32)
    for kv in range(2):
        for j in range(1, n_t):
            piece_copy(kv, j).wait_send()
        for r in (h for h in range(1, nz) if h != half):
            chain_copy(kv, r).wait_send()


def fused(n_dp, n_t, named, cont_len, q, do, ck, cv, pk, pv):
    nz = n_dp // NY
    slots, tokens, width = q.shape
    per, share = pk.shape[:2]
    plen = share * n_t
    dma = pltpu.SemaphoreType.DMA
    shape = jax.ShapeDtypeStruct
    anywhere = pl.BlockSpec(memory_space=pl.ANY)
    scalars = pl.BlockSpec(memory_space=pltpu.SMEM)
    part = shape((per, share, n_t * HD), F32)
    wide = (n_dp, tokens, width)
    tails = (n_dp, 2, tokens, HD)
    pairs = (nz, NY, 2, plen, HD)
    flops = 12 * n_dp * tokens * (tokens + plen) * width
    return pl.pallas_call(
        functools.partial(fused_kernel, n_dp, n_t),
        out_shape=(shape(wide, BF16), shape(wide, BF16), shape(tails, BF16), part, part),
        in_specs=[scalars, scalars] + [anywhere] * 6,
        out_specs=[anywhere] * 3 + [pl.BlockSpec(memory_space=pltpu.VMEM)] * 2,
        scratch_shapes=[pltpu.VMEM((per, plen, HD), BF16) for _ in range(2 * nz)]
        + [
            pltpu.SMEM((3, n_dp), jnp.int32),
            pltpu.VMEM(pairs, BF16),
            pltpu.VMEM(q.shape, BF16),
            pltpu.VMEM(q.shape, BF16),
            pltpu.VMEM(ck.shape, BF16),
            pltpu.VMEM(ck.shape, BF16),
            pltpu.VMEM((n_dp, 2, plen, HD), BF16),
            pltpu.VMEM(wide, BF16),
            pltpu.VMEM(wide, BF16),
            pltpu.VMEM(tails, BF16),
            pltpu.VMEM((n_dp, 2, plen, HD), BF16),
            pltpu.VMEM(pairs, BF16),
            pltpu.VMEM((2, NY, plen, HD), BF16),
            pltpu.VMEM((2, 2, nz, per, plen, HD), BF16),
            pltpu.VMEM((2, per, plen, HD), F32),
            pltpu.VMEM((2, per, plen, HD), BF16),
            pltpu.VMEM((2, n_t, per, share, HD), BF16),
            dma((4,)),
            dma((3, nz)),
            dma((nz, NY, 2)),
            dma((nz, NY, 2)),
            dma((nz, 2)),
            dma((2, NY)),
            dma((2, NY)),
            dma((2, 2, nz)),
            dma((2, 2, nz)),
            dma((2, n_t)),
            dma((2, n_t)),
            dma((2, n_t)),
            dma((2, n_t)),
            dma((2,)),
            dma((2, nz)),
            dma((2, nz)),
            dma((nz, NY, 2)),
            dma((nz, NY, 2)),
        ],
        compiler_params=pltpu.CompilerParams(
            collective_id=0, has_side_effects=True, vmem_limit_bytes=VMEM_LIMIT
        ),
        cost_estimate=pl.CostEstimate(flops=flops, bytes_accessed=4 * q.size * 2, transcendentals=q.size),
        name="fused",
    )(named, cont_len, q, do, ck, cv, pk, pv)


def finish_kernel(per, named_ref, out_ref, dq_ref, tail_ref, k_ref, v_ref, out, dq, dk, dv, gk, gv, ob, dqb, tb, kb, vb, first, last):
    slots = out.shape[0]
    nz = out_ref.shape[0] // NY
    dp = lax.axis_index("dp")
    z, y = dp // NY, dp % NY
    copy = pltpu.make_async_copy
    moved = ((k_ref, kb, gk), (v_ref, vb, gv))

    def fetch(s, w):
        pairs = ((out_ref, ob), (dq_ref, dqb), (tail_ref, tb))
        return [copy(src.at[w], dst.at[s], first.at[i, s]) for i, (src, dst) in enumerate(pairs)]

    def store(s):
        pairs = ((ob, out), (dqb, dq))
        return [copy(src.at[s], dst.at[s], last.at[i, s]) for i, (src, dst) in enumerate(pairs)]

    def begin(s, carry):
        owner = lax.div(named_ref[dp * slots + s], per)
        row = lax.rem(z - owner // NY + nz, nz)
        for c in fetch(s, row * NY + lax.rem(y - owner % NY + NY, NY)):
            c.start()
        return carry

    def pass_on(s, carry):
        for c in fetch(s, 0):
            c.wait()
        for c in store(s):
            c.start()
        return carry

    def end(s, carry):
        for c in store(s):
            c.wait()
        return carry

    lax.fori_loop(0, slots, begin, 0)
    for i, (src, buf, _) in enumerate(moved):
        copy(src, buf, first.at[3, i]).start()
    lax.fori_loop(0, slots, pass_on, 0)
    ends = [copy(tb.at[:, i], dst, last.at[2, i]) for i, dst in enumerate((dk, dv))]
    for i, (src, buf, dst) in enumerate(moved):
        copy(src, buf, first.at[3, i]).wait()
        ends.append(copy(buf, dst, last.at[3, i]))
    for c in ends:
        c.start()
    lax.fori_loop(0, slots, end, 0)
    for c in ends:
        c.wait()


def finish(per, slots, named, out, dq, tail, gk, gv):
    shape = jax.ShapeDtypeStruct
    anywhere = pl.BlockSpec(memory_space=pl.ANY)
    wide = shape((slots,) + out.shape[1:], BF16)
    thin = shape((slots,) + tail.shape[2:], BF16)
    dma = pltpu.SemaphoreType.DMA
    return pl.pallas_call(
        functools.partial(finish_kernel, per),
        out_shape=(wide, wide, thin, thin, shape(gk.shape, F32), shape(gv.shape, F32)),
        in_specs=[pl.BlockSpec(memory_space=pltpu.SMEM)] + [anywhere] * 5,
        out_specs=[anywhere] * 6,
        scratch_shapes=[
            pltpu.VMEM(wide.shape, BF16),
            pltpu.VMEM(wide.shape, BF16),
            pltpu.VMEM((slots,) + tail.shape[1:], BF16),
            pltpu.VMEM(gk.shape, F32),
            pltpu.VMEM(gv.shape, F32),
            dma((4, slots)),
            dma((4, slots)),
        ],
        compiler_params=pltpu.CompilerParams(vmem_limit_bytes=FINISH_LIMIT),
        name="finish",
    )(named, out, dq, tail, gk, gv)


def dot(a, b, dims):
    return lax.dot_general(a, b, (dims, ((), ())), preferred_element_type=F32)


def attend_slot(length, queries, cotangent, keys, values, heads):
    rows = queries.shape[0]
    count = keys.shape[0]
    tokens = rows // heads
    prefix = count - tokens
    scale = 1.0 / math.sqrt(HD)
    token = lax.rem(lax.broadcasted_iota(jnp.int32, (1, rows), 1), tokens)
    valid = lax.rem(lax.broadcasted_iota(jnp.int32, (rows, 1), 0), tokens) < length
    cotangent = jnp.where(valid, cotangent, jnp.zeros_like(cotangent))
    scores = dot(keys, queries, ((1,), (1,)))
    dweights = dot(values, cotangent, ((1,), (1,)))
    key = lax.broadcasted_iota(jnp.int32, (tokens, rows), 0)
    tail = jnp.where(key <= token, scores[prefix:], NEG)
    scores = jnp.concatenate([scores[:prefix], tail], axis=0)
    top = jnp.max(scores, axis=0, keepdims=True)
    exponent = jnp.exp2((scores - top) * (scale * math.log2(math.e)))
    probs = exponent * (1.0 / jnp.sum(exponent, axis=0, keepdims=True))
    weights = probs.astype(BF16)
    delta = jnp.sum(probs * dweights, axis=0, keepdims=True)
    dscores = (probs * ((dweights - delta) * scale)).astype(BF16)
    out = dot(values, weights, ((0,), (0,))).astype(BF16).T
    out = jnp.where(valid, out, jnp.zeros_like(out))
    dq = dot(keys, dscores, ((0,), (0,))).astype(BF16).T
    dk = dot(dscores, queries, ((1,), (0,))).astype(BF16)
    dv = dot(weights, cotangent, ((1,), (0,))).astype(BF16)
    return out, dq, dk, dv


def on_device(n_dp, n_t, cont_q, cont_k, cont_v, out_grad, prompt_k, prompt_v, cont_len, cont_prompt):
    out, dq, tail, gk, gv = fused(
        n_dp, n_t, cont_prompt, cont_len, cont_q, out_grad, cont_k, cont_v, prompt_k, prompt_v
    )
    return finish(prompt_k.shape[0], cont_q.shape[0], cont_prompt, out, dq, tail, gk, gv)


def solution(mesh):
    n_dp, n_t = mesh.shape["dp"], mesh.shape["tensor"]
    return jax.shard_map(
        functools.partial(on_device, n_dp, n_t),
        mesh=mesh,
        in_specs=(
            P("dp", None, "tensor"),
            P("dp", None, "tensor"),
            P("dp", None, "tensor"),
            P("dp", None, "tensor"),
            P("dp", "tensor", None),
            P("dp", "tensor", None),
            P("dp"),
            P(),
        ),
        out_specs=(
            P("dp", None, "tensor"),
            P("dp", None, "tensor"),
            P("dp", None, "tensor"),
            P("dp", None, "tensor"),
            P("dp", "tensor", None),
            P("dp", "tensor", None),
        ),
        check_vma=False,
    )
```
